128 devices in a mesh: lat: 4 (over z), lon: 32 (over y, x, core).
Axes of the slice: x: 4, y: 4, z: 4, core: 2. Of those that a mesh axis runs over, the one named last changes fastest.
Arguments:
- observations: float32 [64, 96, 4096], P('lon', 'lat'), may hold values from 0 to 83
- aux_state: float32 [64, 96, 4096], P('lon', 'lat'), may hold values from -4 to 4
- dual_state: float32 [64, 96, 4096], P('lon', 'lat'), may hold values from -4 to 4
- predictors: float32 [64, 512], replicated, may hold values from -0.25 to 0.25
- inverse_gram: float32 [512, 512], replicated, as said below
Outputs:
- coefficients: float32 [512, 96, 4096], P(None, 'lat', 'lon')
- aux_next: float32 [64, 96, 4096], P('lon', 'lat')
- dual_next: float32 [64, 96, 4096], P('lon', 'lat')
- primal_norm: float32 [], replicated
- dual_norm: float32 [], replicated
The draws below stay inside these ranges and needn't reach their ends.
Inputs may be any that keep to these rules, and one draw needn't show every extreme that they name: `inverse_gram`: symmetric.
All inputs are finite; a program needn't handle non-finite values.
Results may differ from the reference program's by a relative error of at most 0.0003.
Values sent between devices are 32-bit elements; how exact they have to be, the bound alone decides.
No kernel may reach another device: no remote copies, remote signals or barrier semaphores. Data moves between devices by JAX's collectives and lax.ppermute only.
A program may use at most 128 MiB of HBM per device.

```python
import math
import jax
import jax.numpy as jnp
from jax import lax

P_SIZE = 512
LAT_DEV = 24
SWEEPS = 4
DAYS = 64
NLAT = 96
NLON = 4096
N_LAT = 4


def draw_observations(key, part):
    key = jax.random.fold_in(key, 11)
    key_day, key_amount = jax.random.split(key, 2)
    lat_frac = jnp.arange(NLAT, dtype=jnp.float32) / NLAT
    lon_frac = jnp.arange(NLON, dtype=jnp.float32) / NLON
    spatial = 0.2 * jnp.exp(math.log(3.0) * lat_frac)[:, None] * jnp.exp(math.log(10.0) * lon_frac)[None, :]
    day_scale = jnp.exp(jax.random.uniform(key_day, (DAYS, 1, 1), jnp.float32, math.log(0.5), math.log(2.0)))
    amount = -jnp.log(jax.random.uniform(key_amount, (DAYS, NLAT, NLON), jnp.float32, 0.001, 1.0))
    return day_scale * spatial[None, :, :] * amount


def draw_inverse_gram(key, part):
    key = jax.random.fold_in(key, 23)
    key_diag, key_noise = jax.random.split(key, 2)
    diagonal = jax.random.uniform(key_diag, (P_SIZE,), jnp.float32, 0.6, 1.4)
    noise = jax.random.normal(key_noise, (P_SIZE, P_SIZE), jnp.float32)
    symmetric = (noise + noise.T) * (0.2 / math.sqrt(P_SIZE * 1.0))
    return jnp.diag(diagonal) + symmetric


def levels(own_key, extent, shards, smallest, top_value):
    loudness = 1.0
    for dim, parts in shards:
        heights = jax.random.uniform(jax.random.fold_in(jax.random.fold_in(own_key, 6), dim), (parts,), jnp.float32, smallest / len(shards), top_value / len(shards))
        loudness = loudness * jnp.repeat(jnp.exp(heights), extent[dim] // parts).reshape((-1,) + (1,) * (len(extent) - 1 - dim))
    return loudness


def scatter_about(stream_key, dims, deviation, reach, shards=(), kind=jnp.bfloat16):
    values = deviation * jax.random.normal(stream_key, dims, jnp.float32)
    if shards:
        values = values * levels(stream_key, dims, shards, -0.22, 0.18)
    return jnp.clip(values, -reach, reach).astype(kind)


def setup_inputs(seed: int = 0) -> dict:
    keys = jax.random.split(jax.random.key(seed), 6)
    observations = draw_observations(jax.random.fold_in(keys[5], 71), 0)
    aux_state = scatter_about(keys[1], (DAYS, NLAT, NLON), 0.5, 4.0, ((0, 32), (1, 4)), jnp.float32)
    dual_state = scatter_about(keys[2], (DAYS, NLAT, NLON), 0.5, 4.0, ((0, 32), (1, 4)), jnp.float32)
    predictors = scatter_about(keys[3], (DAYS, P_SIZE), P_SIZE ** -0.5, 0.25, (), jnp.float32)
    inverse_gram = draw_inverse_gram(jax.random.fold_in(keys[5], 71), 0)
    return {"observations": observations, "aux_state": aux_state, "dual_state": dual_state, "predictors": predictors, "inverse_gram": inverse_gram}


QUANTILE = 0.9
PENALTY = 2.0
SMOOTHING = 1.0
HIGHEST = lax.Precision.HIGHEST

def estimate(predictors, inverse_gram, target):
    moments = jnp.einsum('dp,dkl->pkl', predictors, target, precision=HIGHEST)
    return jnp.einsum('qp,pkl->qkl', inverse_gram, moments, precision=HIGHEST)

def smooth(beta_hat):
    current = beta_hat
    for step_index in range(SWEEPS):
        padded = jnp.pad(current, ((0, 0), (1, 1), (0, 0)))
        north = padded[:, :-2, :]
        south = padded[:, 2:, :]
        east = jnp.roll(current, -1, axis=2)
        west = jnp.roll(current, 1, axis=2)
        current = (beta_hat + SMOOTHING * (north + south + east + west)) / (1.0 + 4.0 * SMOOTHING)
    return current

def reference(observations, aux_state, dual_state, predictors, inverse_gram):
    target = observations - aux_state + dual_state
    blocks = target.reshape(DAYS, N_LAT, LAT_DEV, NLON).transpose(1, 0, 2, 3)
    beta_hat = lax.map(lambda block: estimate(predictors, inverse_gram, block), blocks)
    beta_hat = beta_hat.transpose(1, 0, 2, 3).reshape(P_SIZE, NLAT, NLON)
    coefficients = smooth(beta_hat)
    fitted = jnp.einsum('dp,pkl->dkl', predictors, coefficients, precision=HIGHEST)
    shifted = observations + dual_state - fitted
    aux_next = shifted - jnp.clip(shifted, -(1.0 - QUANTILE) / PENALTY, QUANTILE / PENALTY)
    dual_next = shifted - aux_next
    primal_diff = dual_next - dual_state
    dual_diff = aux_next - aux_state
    primal_norm = jnp.sqrt(jnp.sum(primal_diff * primal_diff))
    dual_norm = PENALTY * jnp.sqrt(jnp.sum(dual_diff * dual_diff))
    return (coefficients, aux_next, dual_next, primal_norm, dual_norm)
```

```python
import functools

import jax
import jax.numpy as jnp
from jax import lax
from jax.experimental import pallas as pl
from jax.experimental.pallas import tpu as pltpu
from jax.sharding import PartitionSpec as P

SWEEPS = 4
QUANTILE = 0.9
PENALTY = 2.0
SMOOTHING = 1.0
HIGHEST = lax.Precision.HIGHEST
HALO = 4
LANES = 128
PARAMS = pltpu.CompilerParams(vmem_limit_bytes=48 * 2**20)


def call(kernel, outs, flops=0, bytes_accessed=0, scratch=()):
    return pl.pallas_call(
        kernel,
        out_shape=outs,
        scratch_shapes=scratch,
        compiler_params=PARAMS,
        cost_estimate=pl.CostEstimate(flops=flops, bytes_accessed=bytes_accessed, transcendentals=0),
    )


def sublanes(shape):
    return lax.broadcasted_iota(jnp.int32, shape, 0)


def edges_kernel(obs, aux, dual, top, bottom):
    low = sublanes((8, obs.shape[2])) < HALO
    last = obs.shape[1] - 8

    def target(day, row):
        rows = pl.ds(row, 8)
        return obs[day, rows, :] - aux[day, rows, :] + dual[day, rows, :]

    top[...] = jnp.where(low, target(0, 0), pltpu.roll(target(1, 0), HALO, 0))
    bottom[...] = jnp.where(low, pltpu.roll(target(1, last), HALO, 0), target(0, last))


def smooth_kernel(lat_count, obs, aux, dual, below, above, out, base, first, second):
    blocks, days, rows, _ = out.shape
    lat = lax.axis_index("lat")
    low = sublanes((8, LANES)) < HALO
    inside = jnp.where(low, jnp.where(lat < lat_count - 1, 1.0, 0.0), jnp.where(lat > 0, 1.0, 0.0))
    total = rows + 8
    keep = jnp.concatenate([jnp.ones((rows, LANES), jnp.float32), inside], axis=0)
    lane = lax.broadcasted_iota(jnp.int32, (total, LANES), 1)
    for day in range(days):
        for j in range(blocks):
            cols = pl.ds(j * LANES, LANES)
            own = obs[day, :, cols] - aux[day, :, cols] + dual[day, :, cols]
            if day == 0:
                ghost = jnp.where(low, below[:, cols], above[:, cols])
            else:
                ghost = pltpu.roll(jnp.where(low, above[:, cols], below[:, cols]), HALO, 0)
            base[j] = jnp.concatenate([own, ghost], axis=0)
        source = base
        for sweep in range(SWEEPS):
            final = sweep == SWEEPS - 1
            target = first if sweep % 2 == 0 else second
            for j in range(blocks):
                now = source[j]
                left = source[(j - 1) % blocks]
                right = source[(j + 1) % blocks]
                west = jnp.where(lane == 0, pltpu.roll(left, 1, 1), pltpu.roll(now, 1, 1))
                east = jnp.where(lane == LANES - 1, pltpu.roll(right, LANES - 1, 1), pltpu.roll(now, LANES - 1, 1))
                beside = pltpu.roll(now, 1, 0) + pltpu.roll(now, total - 1, 0) + east + west
                new = (base[j] + SMOOTHING * beside) * (1.0 / (1.0 + 4.0 * SMOOTHING))
                if final:
                    out[j, day] = new[:rows]
                else:
                    target[j] = new * keep
            source = target


def split(x):
    high = x.astype(jnp.bfloat16)
    return high, (x - high.astype(jnp.float32)).astype(jnp.bfloat16)


def stack_left(matrix):
    high, low = split(matrix)
    return jnp.concatenate([high, low, high], axis=1)


def fitted_kernel(smooth, matrix, fitted, stacked):
    days, rows, _ = smooth.shape
    left = stack_left(matrix[...])
    for r in range(rows):
        high, low = split(smooth[:, r, :])
        right = jnp.concatenate([high, high, low], axis=0)
        stacked[r] = right
        fitted[:, r, :] = jnp.dot(left, right, preferred_element_type=jnp.float32)


def coefficients_kernel(stacked, matrix, out):
    left = stack_left(matrix[...])
    for r in range(out.shape[1]):
        out[:, r, :] = jnp.dot(left, stacked[r], preferred_element_type=jnp.float32)


def proximal_kernel(peers, obs, aux, dual, fitted, aux_next, dual_next, sums):
    blocks, days, rows, _ = fitted.shape
    primal = jnp.zeros((rows, LANES), jnp.float32)
    change = jnp.zeros((rows, LANES), jnp.float32)
    for day in range(days):
        for j in range(blocks):
            cols = pl.ds(j * LANES, LANES)
            dual_now = dual[day, :, cols]
            shifted = obs[day, :, cols] + dual_now - fitted[j, day]
            aux_new = shifted - jnp.clip(shifted, -(1.0 - QUANTILE) / PENALTY, QUANTILE / PENALTY)
            dual_new = shifted - aux_new
            aux_next[day, :, cols] = aux_new
            dual_next[day, :, cols] = dual_new
            primal += (dual_new - dual_now) * (dual_new - dual_now)
            moved = aux_new - aux[day, :, cols]
            change += moved * moved
    both = jnp.concatenate([jnp.sum(primal, axis=0, keepdims=True), jnp.sum(change, axis=0, keepdims=True)], axis=0)
    sums[...] = jnp.broadcast_to(both[None], sums.shape)


def f32(*shape):
    return jax.ShapeDtypeStruct(shape, jnp.float32)


def local(lat_count, lon_count, observations, aux_state, dual_state, predictors, inverse_gram):
    days, rows, columns = observations.shape
    blocks = columns // LANES
    all_days = days * lon_count
    cells = days * rows * columns
    top, bottom = call(edges_kernel, (f32(8, columns), f32(8, columns)), 4 * cells, 8 * cells)(
        observations, aux_state, dual_state
    )
    north = [(i + 1, i) for i in range(lat_count - 1)]
    south = [(i, i + 1) for i in range(lat_count - 1)]
    below = lax.ppermute(top, "lat", north)
    above = lax.ppermute(bottom, "lat", south)
    smooth = call(
        functools.partial(smooth_kernel, lat_count),
        f32(blocks, days, rows, LANES),
        64 * cells,
        16 * cells,
        [pltpu.VMEM((blocks, rows + 8, LANES), jnp.float32)] * 3,
    )(observations, aux_state, dual_state, below, above)
    smooth = lax.all_to_all(smooth, "lon", 0, 0, tiled=True).reshape(all_days, rows, LANES)

    to_coefficients = jnp.einsum("qp,dp->qd", inverse_gram, predictors, precision=HIGHEST)
    to_fitted = jnp.einsum("dp,pe->de", predictors, to_coefficients, precision=HIGHEST)
    fitted, stacked = call(
        fitted_kernel,
        (f32(all_days, rows, LANES), jax.ShapeDtypeStruct((rows, 3 * all_days, LANES), jnp.bfloat16)),
        6 * all_days * cells,
        12 * cells,
    )(smooth, to_fitted)
    fitted = lax.all_to_all(fitted.reshape(lon_count, days, rows, LANES), "lon", 0, 0, tiled=True)
    coefficients = call(
        coefficients_kernel,
        f32(to_coefficients.shape[0], rows, LANES),
        6 * 512 * cells,
        4 * 512 * rows * LANES,
    )(stacked, to_coefficients)
    devices = lat_count * lon_count
    aux_next, dual_next, sums = call(
        functools.partial(proximal_kernel, devices),
        (f32(days, rows, columns), f32(days, rows, columns), f32(devices, 2, LANES)),
        10 * cells,
        24 * cells,
    )(observations, aux_state, dual_state, fitted)
    sums = lax.all_to_all(sums, ("lat", "lon"), 0, 0, tiled=True)
    totals = jnp.sum(sums, axis=(0, 2))
    return (coefficients, aux_next, dual_next, jnp.sqrt(totals[0]), PENALTY * jnp.sqrt(totals[1]))


def solution(mesh):
    in_specs = (P("lon", "lat", None), P("lon", "lat", None), P("lon", "lat", None), P(), P())
    out_specs = (P(None, "lat", "lon"), P("lon", "lat", None), P("lon", "lat", None), P(), P())
    body = functools.partial(local, mesh.shape["lat"], mesh.shape["lon"])
    return jax.shard_map(body, mesh=mesh, in_specs=in_specs, out_specs=out_specs, check_vma=False)
```

```python
import functools
import math

import jax
import jax.numpy as jnp
import numpy as np
from jax import lax
from jax.experimental import pallas as pl
from jax.experimental.pallas import tpu as pltpu
from jax.sharding import PartitionSpec as P

SWEEPS = 4
QUANTILE = 0.9
PENALTY = 2.0
SMOOTHING = 1.0
HIGHEST = lax.Precision.HIGHEST
HALO = 4
LANES = 128
TILE = 8
UNROLL = 8
PARTS = 8
EDGES_MIB = 52.5
SCALE = 1.0 / 625.0
IN_VMEM = pl.BlockSpec(memory_space=pltpu.VMEM)
IN_HBM = pl.BlockSpec(memory_space=pltpu.HBM)
DMA = pltpu.SemaphoreType.DMA


def f32(*shape):
    return jax.ShapeDtypeStruct(shape, jnp.float32)


def bf16(*shape):
    return jax.ShapeDtypeStruct(shape, jnp.bfloat16)


def call(kernel, outs, in_specs, out_specs, us, scratch=(), mib=20):
    return pl.pallas_call(
        kernel,
        out_shape=outs,
        in_specs=in_specs,
        out_specs=out_specs,
        scratch_shapes=scratch,
        compiler_params=pltpu.CompilerParams(vmem_limit_bytes=int(mib * 2**20)),
        cost_estimate=pl.CostEstimate(flops=int(us * 1e9), bytes_accessed=0, transcendentals=0),
    )


def iota(shape, dim):
    return lax.broadcasted_iota(jnp.int32, shape, dim)


def columns_operator():
    powers = [np.array([1.0])]
    for _ in range(SWEEPS):
        powers.append(np.convolve(powers[-1], [1.0, 0.0, 1.0]))
    weights = [5.0 ** (SWEEPS - 1 - j) for j in range(SWEEPS)] + [1.0]
    inner = np.zeros((LANES, SWEEPS, LANES))
    outer = np.zeros((LANES, SWEEPS, LANES))
    for k in range(SWEEPS):
        band = np.zeros(2 * SWEEPS + 1)
        for j in range(k, SWEEPS + 1):
            reach = j - k
            band[SWEEPS - reach : SWEEPS + reach + 1] += weights[j] * math.comb(j, k) * powers[reach]
        for lane in range(LANES):
            for step in range(-SWEEPS, SWEEPS + 1):
                source = lane + step
                into = inner if 0 <= source < LANES else outer
                into[source % LANES, k, lane] = band[SWEEPS + step]
    inner, outer = (part.reshape(LANES, SWEEPS * LANES) for part in (inner, outer))
    return np.concatenate([inner, inner, outer, outer], axis=0)


def edges_kernel(obs, aux, dual, target, top, bottom, held, sems):
    days, rows, _ = obs.shape
    copies = []
    for day in range(days):
        for k, array in enumerate((obs, aux, dual)):
            copies.append(pltpu.make_async_copy(array.at[day], held.at[day, k], sems.at[day, k]))
    for copy in copies:
        copy.start()
    for day in range(days):
        for k in range(3):
            copies[day * 3 + k].wait()
        target[day] = held[day, 0] - held[day, 1] + held[day, 2]
    low = iota(top.shape, 0) < HALO
    last = rows - TILE
    top[...] = jnp.where(low, target[0, :TILE], pltpu.roll(target[1, :TILE], HALO, 0))
    bottom[...] = jnp.where(low, pltpu.roll(target[1, last:], HALO, 0), target[0, last:])


def split(x):
    high = x.astype(jnp.bfloat16)
    return high, (x - high.astype(jnp.float32)).astype(jnp.bfloat16)


def columns_part(blocks, operator):
    first = iota(blocks[0].shape, 1) < LANES // 2
    stacked = []
    for u in range(1, len(blocks) - 1):
        beside = jnp.where(first, blocks[u + 1], blocks[u - 1])
        stacked.append(jnp.concatenate(split(blocks[u]) + split(beside), axis=1))
    return jnp.dot(jnp.concatenate(stacked, axis=0), operator[...], preferred_element_type=jnp.float32)


def own_kernel(lat_count, target, operator, out):
    blocks, days, rows, _ = out.shape
    lat = lax.axis_index("lat")
    total = rows + TILE
    low = iota((TILE, LANES), 0) < HALO
    inside = jnp.where(low, jnp.where(lat < lat_count - 1, 1.0, 0.0), jnp.where(lat > 0, 1.0, 0.0))
    zero = jnp.zeros((TILE, LANES), jnp.float32)

    def body(group, carry):
        start = group * UNROLL
        held = []
        for u in range(-1, UNROLL + 1):
            j = lax.rem(start + u + blocks, blocks)
            cols = pl.ds(pl.multiple_of(j * LANES, LANES), LANES)
            held.append(jnp.concatenate([target[day, :, cols] for day in range(days)], axis=0))
        parts = columns_part(held, operator)
        for u in range(UNROLL):
            for day in range(days):
                at = (u * days + day) * rows
                now = jnp.concatenate([held[u + 1][day * rows : (day + 1) * rows], zero], axis=0)
                for k in reversed(range(SWEEPS)):
                    upright = pltpu.roll(now, 1, 0) + pltpu.roll(now, total - 1, 0)
                    new = upright[:rows] + parts[at : at + rows, k * LANES : (k + 1) * LANES]
                    if k:
                        now = jnp.concatenate([new, upright[rows:] * inside], axis=0)
                out[start + u, day] = new * SCALE
        return carry

    lax.fori_loop(0, blocks // UNROLL, body, 0)


def halo_kernel(lat_count, own, below, above, operator, after, out):
    blocks, days, rows, _ = own.shape
    row = iota((TILE, LANES), 0)
    low = row < HALO
    begin, end = row == 0, row == TILE - 1
    zero = jnp.zeros((TILE, LANES), jnp.float32)
    lat = lax.axis_index("lat")
    south_scale = jnp.where(lat < lat_count - 1, SCALE, 0.0)
    north_scale = jnp.where(lat > 0, SCALE, 0.0)

    def spread(south, north):
        return (
            (jnp.where(low, pltpu.roll(north, HALO, 0), zero), jnp.where(low, zero, pltpu.roll(south, HALO, 0))),
            (jnp.where(low, north, zero), jnp.where(low, zero, south)),
        )

    def body(group, carry):
        start = group * UNROLL
        held = []
        for u in range(-1, UNROLL + 1):
            j = lax.rem(start + u + blocks, blocks)
            cols = pl.ds(pl.multiple_of(j * LANES, LANES), LANES)
            held.append(jnp.concatenate([below[:, cols], above[:, cols]], axis=0))
        parts = columns_part(held, operator)
        for u in range(UNROLL):
            at = u * 2 * TILE
            now = spread(held[u + 1][:TILE], held[u + 1][TILE:])
            for k in reversed(range(SWEEPS)):
                cols = slice(k * LANES, (k + 1) * LANES)
                part = spread(parts[at : at + TILE, cols], parts[at + TILE : at + 2 * TILE, cols])
                now = tuple(
                    tuple(
                        jnp.where(begin, zero, pltpu.roll(now[day][side], 1, 0))
                        + jnp.where(end, zero, pltpu.roll(now[day][side], TILE - 1, 0))
                        + part[day][side]
                        for side in range(2)
                    )
                    for day in range(days)
                )
            j = start + u
            for day in range(days):
                north = pltpu.roll(now[day][0], HALO, 0) * north_scale
                south = pltpu.roll(now[day][1], HALO, 0) * south_scale
                out[j, day, :TILE] = own[j, day, :TILE] + jnp.where(low, north, zero)
                out[j, day, TILE : rows - TILE] = own[j, day, TILE : rows - TILE]
                out[j, day, rows - TILE :] = own[j, day, rows - TILE :] + jnp.where(low, zero, south)
        return carry

    lax.fori_loop(0, blocks // UNROLL, body, 0)


def stack_left(matrix):
    high, low = split(matrix)
    return jnp.concatenate([high, low, high], axis=1)


def maps_kernel(predictors, inverse_gram, to_coefficients, to_fitted):
    scores = predictors[...]
    contract = (((1,), (1,)), ((), ()))
    direct = lax.dot_general(
        inverse_gram[...], scores, contract, precision=HIGHEST, preferred_element_type=jnp.float32
    )
    back = jnp.dot(scores, direct, precision=HIGHEST, preferred_element_type=jnp.float32)
    to_coefficients[...] = stack_left(direct)
    to_fitted[...] = stack_left(back)


def pairs(smooth, rows, days):
    for r in range(0, rows, 2):
        high, low = split(jnp.concatenate([smooth[pl.ds(r + i, days, stride=rows), :] for i in range(2)], axis=1))
        yield r, jnp.concatenate([high, high, low], axis=0)


def fitted_kernel(smooth, matrix, fitted):
    days = matrix.shape[0]
    rows = smooth.shape[0] // days
    for r, right in pairs(smooth, rows, days):
        both = jnp.dot(matrix[...], right, preferred_element_type=jnp.float32)
        for i in range(2):
            fitted[pl.ds(r + i, days, stride=rows), :] = both[:, i * LANES : (i + 1) * LANES]


def proximal(obs, dual, fitted):
    shifted = obs + dual - fitted
    auxiliary = shifted - jnp.clip(shifted, -(1.0 - QUANTILE) / PENALTY, QUANTILE / PENALTY)
    return auxiliary, shifted - auxiliary


def sums_kernel(obs, aux, dual, fitted, sums):
    blocks, days, rows, _ = fitted.shape

    def body(group, carry):
        primal, change = carry
        for u in range(UNROLL):
            j = group * UNROLL + u
            cols = pl.ds(pl.multiple_of(j * LANES, LANES), LANES)
            for day in range(days):
                dual_now = dual[day, :, cols]
                aux_new, dual_new = proximal(obs[day, :, cols], dual_now, fitted[j, day])
                moved = dual_new - dual_now
                primal += moved * moved
                moved = aux_new - aux[day, :, cols]
                change += moved * moved
        return primal, change

    zero = jnp.zeros((rows, LANES), jnp.float32)
    primal, change = lax.fori_loop(0, blocks // UNROLL, body, (zero, zero))
    primal = jnp.sum(primal, axis=0, keepdims=True)
    change = jnp.sum(change, axis=0, keepdims=True)
    half = LANES // 2
    both = jnp.where(
        iota((1, LANES), 1) < half, primal + pltpu.roll(primal, half, 1), change + pltpu.roll(change, half, 1)
    )
    sums[...] = jnp.broadcast_to(both[None], sums.shape)


def results_kernel(
    smooth, matrix, obs, dual, fitted, after, coefficients, aux_next, dual_next, stacked, held, aux_held, dual_held, sems
):
    depth = matrix.shape[0]
    days_all = matrix.shape[1] // 3
    blocks, days, rows, _ = fitted.shape
    part = depth // PARTS
    copies = []

    def send(source, target, k):
        copies.append(pltpu.make_async_copy(source, target, sems.at[k]))
        copies[-1].start()

    for r, right in pairs(smooth, rows, days_all):
        stacked[r // 2] = right
    for k in range(PARTS):
        for r in range(0, rows, 2):
            both = jnp.dot(
                matrix[k * part : (k + 1) * part, :], stacked[r // 2], preferred_element_type=jnp.float32
            )
            for i in range(2):
                held[pl.ds(k * part * rows + r + i, part, stride=rows), :] = both[:, i * LANES : (i + 1) * LANES]
        span = pl.ds(k * part * rows, part * rows)
        send(held.at[span], coefficients.at[span], k)

    for day in range(days):

        def body(group, carry):
            for u in range(UNROLL):
                j = group * UNROLL + u
                cols = pl.ds(pl.multiple_of(j * LANES, LANES), LANES)
                aux_new, dual_new = proximal(obs[day, :, cols], dual[day, :, cols], fitted[j, day])
                aux_held[day, :, cols] = aux_new
                dual_held[day, :, cols] = dual_new
            return carry

        lax.fori_loop(0, blocks // UNROLL, body, 0)
        send(aux_held.at[day], aux_next.at[day], PARTS + day)
        send(dual_held.at[day], dual_next.at[day], PARTS + days + day)
    for copy in copies:
        copy.wait()


def norms_kernel(sums, primal, change):
    row = jnp.sum(sums[...], axis=0)
    half = iota(row.shape, 1) < LANES // 2
    primal[...] = jnp.sqrt(jnp.sum(jnp.where(half, row, 0.0), axis=1, keepdims=True))
    change[...] = PENALTY * jnp.sqrt(jnp.sum(jnp.where(half, 0.0, row), axis=1, keepdims=True))


def local(lat_count, lon_count, observations, aux_state, dual_state, predictors, inverse_gram):
    days, rows, columns = observations.shape
    blocks = columns // LANES
    all_days = days * lon_count
    depth = inverse_gram.shape[0]
    field = f32(blocks, days, rows, LANES)
    state = (observations, aux_state, dual_state)
    slab = f32(days, rows, columns)
    tile = f32(TILE, columns)
    target, top, bottom = call(
        edges_kernel,
        (slab, tile, tile),
        [IN_HBM] * 3,
        (IN_VMEM,) * 3,
        2.0,
        [pltpu.VMEM((days, 3, rows, columns), jnp.float32), DMA((days, 3))],
        EDGES_MIB,
    )(*state)
    below = lax.ppermute(top, "lat", [((i + 1) % lat_count, i) for i in range(lat_count)])
    above = lax.ppermute(bottom, "lat", [(i, (i + 1) % lat_count) for i in range(lat_count)])
    operator = jnp.asarray(columns_operator(), jnp.bfloat16)
    own = call(functools.partial(own_kernel, lat_count), field, [IN_VMEM] * 2, IN_VMEM, 3.0)(target, operator)
    to_coefficients, to_fitted = call(
        maps_kernel,
        (bf16(depth, 3 * all_days), bf16(all_days, 3 * all_days)),
        [IN_VMEM] * 2,
        (IN_VMEM, IN_VMEM),
        2.0,
    )(predictors, inverse_gram)
    smooth = call(functools.partial(halo_kernel, lat_count), field, [IN_VMEM] * 5, IN_VMEM, 1.5)(
        own, below, above, operator, to_fitted
    )
    smooth = lax.all_to_all(smooth, "lon", 0, 0, tiled=True).reshape(all_days * rows, LANES)
    fitted = call(fitted_kernel, f32(all_days * rows, LANES), [IN_VMEM] * 2, IN_VMEM, 2.0)(smooth, to_fitted)
    fitted = lax.all_to_all(fitted.reshape(field.shape), "lon", 0, 0, tiled=True)
    devices = lat_count * lon_count
    sums = call(sums_kernel, f32(devices, 1, LANES), [IN_VMEM] * 4, IN_VMEM, 1.0)(
        *state, fitted
    )
    coefficients, aux_next, dual_next = call(
        results_kernel,
        (f32(depth * rows, LANES), slab, slab),
        [IN_VMEM] * 5 + [IN_HBM],
        (IN_HBM,) * 3,
        5.0,
        [
            pltpu.VMEM((rows // 2, 3 * all_days, 2 * LANES), jnp.bfloat16),
            pltpu.VMEM((depth * rows, LANES), jnp.float32),
            pltpu.VMEM(slab.shape, jnp.float32),
            pltpu.VMEM(slab.shape, jnp.float32),
            DMA((PARTS + 2 * days,)),
        ],
    )(smooth, to_coefficients, observations, dual_state, fitted, sums)
    coefficients = coefficients.reshape(depth, rows, LANES)
    sums = lax.all_to_all(sums, ("lat", "lon"), 0, 0, tiled=True)
    primal, change = call(norms_kernel, (f32(1, 1), f32(1, 1)), [IN_VMEM], (IN_VMEM, IN_VMEM), 0.5)(sums)
    return (coefficients, aux_next, dual_next, primal.reshape(()), change.reshape(()))


def solution(mesh):
    in_specs = (P("lon", "lat", None), P("lon", "lat", None), P("lon", "lat", None), P(), P())
    out_specs = (P(None, "lat", "lon"), P("lon", "lat", None), P("lon", "lat", None), P(), P())
    body = functools.partial(local, mesh.shape["lat"], mesh.shape["lon"])
    return jax.shard_map(body, mesh=mesh, in_specs=in_specs, out_specs=out_specs, check_vma=False)
```

```python
import functools
import math

import jax
import jax.numpy as jnp
import numpy as np
from jax import lax
from jax.experimental import pallas as pl
from jax.experimental.pallas import tpu as pltpu
from jax.sharding import PartitionSpec as P

SWEEPS = 4
QUANTILE = 0.9
PENALTY = 2.0
SMOOTHING = 1.0
HIGHEST = lax.Precision.HIGHEST
HALO = 4
LANES = 128
TILE = 8
UNROLL = 8
OWN_UNROLL = 32
HALO_UNROLL = 32
PARTS = 8
EDGES_MIB = 52.5
SCALE = 1.0 / 625.0
IN_VMEM = pl.BlockSpec(memory_space=pltpu.VMEM)
IN_HBM = pl.BlockSpec(memory_space=pltpu.HBM)
DMA = pltpu.SemaphoreType.DMA


def f32(*shape):
    return jax.ShapeDtypeStruct(shape, jnp.float32)


def bf16(*shape):
    return jax.ShapeDtypeStruct(shape, jnp.bfloat16)


def call(kernel, outs, in_specs, out_specs, us, scratch=(), mib=20):
    return pl.pallas_call(
        kernel,
        out_shape=outs,
        in_specs=in_specs,
        out_specs=out_specs,
        scratch_shapes=scratch,
        compiler_params=pltpu.CompilerParams(vmem_limit_bytes=int(mib * 2**20)),
        cost_estimate=pl.CostEstimate(flops=int(us * 1e9), bytes_accessed=0, transcendentals=0),
    )


def iota(shape, dim):
    return lax.broadcasted_iota(jnp.int32, shape, dim)


def columns_operator():
    powers = [np.array([1.0])]
    for _ in range(SWEEPS):
        powers.append(np.convolve(powers[-1], [1.0, 0.0, 1.0]))
    weights = [5.0 ** (SWEEPS - 1 - j) for j in range(SWEEPS)] + [1.0]
    inner = np.zeros((LANES, SWEEPS, LANES))
    outer = np.zeros((LANES, SWEEPS, LANES))
    for k in range(SWEEPS):
        band = np.zeros(2 * SWEEPS + 1)
        for j in range(k, SWEEPS + 1):
            reach = j - k
            band[SWEEPS - reach : SWEEPS + reach + 1] += weights[j] * math.comb(j, k) * powers[reach]
        for lane in range(LANES):
            for step in range(-SWEEPS, SWEEPS + 1):
                source = lane + step
                into = inner if 0 <= source < LANES else outer
                into[source % LANES, k, lane] = band[SWEEPS + step]
    inner, outer = (part.reshape(LANES, SWEEPS * LANES) for part in (inner, outer))
    return np.concatenate([inner, inner, outer, outer], axis=0)


def edges_kernel(obs, aux, dual, target, bottom, top, held, sems):
    days, rows, _ = obs.shape
    copies = []
    for day in range(days):
        for k, array in enumerate((obs, aux, dual)):
            copies.append(pltpu.make_async_copy(array.at[day], held.at[day, k], sems.at[day, k]))
    for copy in copies:
        copy.start()
    for day in range(days):
        for k in range(3):
            copies[day * 3 + k].wait()
        target[day] = held[day, 0] - held[day, 1] + held[day, 2]
    low = iota(top.shape, 0) < HALO
    last = rows - TILE
    top[...] = jnp.where(low, target[0, :TILE], pltpu.roll(target[1, :TILE], HALO, 0))
    bottom[...] = jnp.where(low, pltpu.roll(target[1, last:], HALO, 0), target[0, last:])


def split(x):
    high = x.astype(jnp.bfloat16)
    return high, (x - high.astype(jnp.float32)).astype(jnp.bfloat16)


def columns_part(blocks, operator):
    first = iota(blocks[0].shape, 1) < LANES // 2
    stacked = []
    for u in range(1, len(blocks) - 1):
        beside = jnp.where(first, blocks[u + 1], blocks[u - 1])
        stacked.append(jnp.concatenate(split(blocks[u]) + split(beside), axis=1))
    return jnp.dot(jnp.concatenate(stacked, axis=0), operator[...], preferred_element_type=jnp.float32)


def own_kernel(lat_count, target, operator, out):
    blocks, days, rows, _ = out.shape
    lat = lax.axis_index("lat")
    total = rows + TILE
    low = iota((TILE, LANES), 0) < HALO
    inside = jnp.where(low, jnp.where(lat < lat_count - 1, 1.0, 0.0), jnp.where(lat > 0, 1.0, 0.0))
    zero = jnp.zeros((TILE, LANES), jnp.float32)

    def body(group, carry):
        start = group * OWN_UNROLL
        held = []
        for u in range(-1, OWN_UNROLL + 1):
            j = lax.rem(start + u + blocks, blocks)
            cols = pl.ds(pl.multiple_of(j * LANES, LANES), LANES)
            held.append(jnp.concatenate([target[day, :, cols] for day in range(days)], axis=0))
        parts = columns_part(held, operator)
        for u in range(OWN_UNROLL):
            for day in range(days):
                at = (u * days + day) * rows
                now = jnp.concatenate([held[u + 1][day * rows : (day + 1) * rows], zero], axis=0)
                for k in reversed(range(SWEEPS)):
                    upright = pltpu.roll(now, 1, 0) + pltpu.roll(now, total - 1, 0)
                    new = upright[:rows] + parts[at : at + rows, k * LANES : (k + 1) * LANES]
                    if k:
                        now = jnp.concatenate([new, upright[rows:] * inside], axis=0)
                out[start + u, day] = new * SCALE
        return carry

    lax.fori_loop(0, blocks // OWN_UNROLL, body, 0)


def halo_kernel(lat_count, own, above, below, operator, after, out):
    blocks, days, rows, _ = own.shape
    row = iota((TILE, LANES), 0)
    low = row < HALO
    begin, end = row == 0, row == TILE - 1
    zero = jnp.zeros((TILE, LANES), jnp.float32)
    lat = lax.axis_index("lat")
    south_scale = jnp.where(lat < lat_count - 1, SCALE, 0.0)
    north_scale = jnp.where(lat > 0, SCALE, 0.0)

    def spread(south, north):
        return (
            (jnp.where(low, pltpu.roll(north, HALO, 0), zero), jnp.where(low, zero, pltpu.roll(south, HALO, 0))),
            (jnp.where(low, north, zero), jnp.where(low, zero, south)),
        )

    def body(group, carry):
        start = group * HALO_UNROLL
        held = []
        for u in range(-1, HALO_UNROLL + 1):
            j = lax.rem(start + u + blocks, blocks)
            cols = pl.ds(pl.multiple_of(j * LANES, LANES), LANES)
            held.append(jnp.concatenate([below[:, cols], above[:, cols]], axis=0))
        parts = columns_part(held, operator)
        for u in range(HALO_UNROLL):
            at = u * 2 * TILE
            now = spread(held[u + 1][:TILE], held[u + 1][TILE:])
            for k in reversed(range(SWEEPS)):
                cols = slice(k * LANES, (k + 1) * LANES)
                part = spread(parts[at : at + TILE, cols], parts[at + TILE : at + 2 * TILE, cols])
                now = tuple(
                    tuple(
                        jnp.where(begin, zero, pltpu.roll(now[day][side], 1, 0))
                        + jnp.where(end, zero, pltpu.roll(now[day][side], TILE - 1, 0))
                        + part[day][side]
                        for side in range(2)
                    )
                    for day in range(days)
                )
            j = start + u
            for day in range(days):
                north = pltpu.roll(now[day][0], HALO, 0) * north_scale
                south = pltpu.roll(now[day][1], HALO, 0) * south_scale
                out[j, day, :TILE] = own[j, day, :TILE] + jnp.where(low, north, zero)
                out[j, day, TILE : rows - TILE] = own[j, day, TILE : rows - TILE]
                out[j, day, rows - TILE :] = own[j, day, rows - TILE :] + jnp.where(low, zero, south)
        return carry

    lax.fori_loop(0, blocks // HALO_UNROLL, body, 0)


def stack_left(matrix):
    high, low = split(matrix)
    return jnp.concatenate([high, low, high], axis=1)


def stack_right(matrix):
    high, low = split(matrix)
    return jnp.concatenate([high, high, low], axis=0)


def maps_kernel(predictors, inverse_gram, to_coefficients, to_fitted):
    scores = predictors[...]
    direct = jnp.dot(stack_left(inverse_gram[...]), stack_right(scores.T), preferred_element_type=jnp.float32)
    back = jnp.dot(stack_left(scores), stack_right(direct), preferred_element_type=jnp.float32)
    to_coefficients[...] = stack_left(direct)
    to_fitted[...] = stack_left(back)


def pairs(smooth, rows, days):
    for r in range(0, rows, 2):
        high, low = split(jnp.concatenate([smooth[pl.ds(r + i, days, stride=rows), :] for i in range(2)], axis=1))
        yield r, jnp.concatenate([high, high, low], axis=0)


def fitted_kernel(smooth, matrix, fitted):
    days = matrix.shape[0]
    rows = smooth.shape[0] // days
    for r, right in pairs(smooth, rows, days):
        both = jnp.dot(matrix[...], right, preferred_element_type=jnp.float32)
        for i in range(2):
            fitted[pl.ds(r + i, days, stride=rows), :] = both[:, i * LANES : (i + 1) * LANES]


def proximal(obs, dual, fitted):
    shifted = obs + dual - fitted
    auxiliary = shifted - jnp.clip(shifted, -(1.0 - QUANTILE) / PENALTY, QUANTILE / PENALTY)
    return auxiliary, shifted - auxiliary


def sums_kernel(obs, aux, dual, fitted, sums):
    blocks, days, rows, _ = fitted.shape

    def body(group, carry):
        primal, change = carry
        for u in range(UNROLL):
            j = group * UNROLL + u
            cols = pl.ds(pl.multiple_of(j * LANES, LANES), LANES)
            for day in range(days):
                dual_now = dual[day, :, cols]
                aux_new, dual_new = proximal(obs[day, :, cols], dual_now, fitted[j, day])
                moved = dual_new - dual_now
                primal += moved * moved
                moved = aux_new - aux[day, :, cols]
                change += moved * moved
        return primal, change

    zero = jnp.zeros((rows, LANES), jnp.float32)
    primal, change = lax.fori_loop(0, blocks // UNROLL, body, (zero, zero))
    primal = jnp.sum(primal, axis=0, keepdims=True)
    change = jnp.sum(change, axis=0, keepdims=True)
    half = LANES // 2
    both = jnp.where(
        iota((1, LANES), 1) < half, primal + pltpu.roll(primal, half, 1), change + pltpu.roll(change, half, 1)
    )
    sums[...] = jnp.broadcast_to(both[None], sums.shape)


def results_kernel(
    smooth, matrix, obs, dual, fitted, after, coefficients, aux_next, dual_next, stacked, held, aux_held, dual_held, sems
):
    depth = matrix.shape[0]
    days_all = matrix.shape[1] // 3
    blocks, days, rows, _ = fitted.shape
    part = depth // PARTS
    copies = []

    def send(source, target, k):
        copies.append(pltpu.make_async_copy(source, target, sems.at[k]))
        copies[-1].start(priority=k % 2)

    for r, right in pairs(smooth, rows, days_all):
        stacked[r // 2] = right
    for k in range(PARTS):
        for r in range(0, rows, 2):
            both = jnp.dot(
                matrix[k * part : (k + 1) * part, :], stacked[r // 2], preferred_element_type=jnp.float32
            )
            for i in range(2):
                held[pl.ds(k * part * rows + r + i, part, stride=rows), :] = both[:, i * LANES : (i + 1) * LANES]
        span = pl.ds(k * part * rows, part * rows)
        send(held.at[span], coefficients.at[span], k)

    for day in range(days):

        def body(group, carry):
            for u in range(UNROLL):
                j = group * UNROLL + u
                cols = pl.ds(pl.multiple_of(j * LANES, LANES), LANES)
                aux_new, dual_new = proximal(obs[day, :, cols], dual[day, :, cols], fitted[j, day])
                aux_held[day, :, cols] = aux_new
                dual_held[day, :, cols] = dual_new
            return carry

        lax.fori_loop(0, blocks // UNROLL, body, 0)
        send(aux_held.at[day], aux_next.at[day], PARTS + day)
        send(dual_held.at[day], dual_next.at[day], PARTS + days + day)
    for copy in copies:
        copy.wait()


def norms_kernel(sums, primal, change):
    row = jnp.sum(sums[...], axis=0)
    half = iota(row.shape, 1) < LANES // 2
    primal[...] = jnp.sqrt(jnp.sum(jnp.where(half, row, 0.0), axis=1, keepdims=True))
    change[...] = PENALTY * jnp.sqrt(jnp.sum(jnp.where(half, 0.0, row), axis=1, keepdims=True))


def local(lat_count, lon_count, observations, aux_state, dual_state, predictors, inverse_gram):
    days, rows, columns = observations.shape
    blocks = columns // LANES
    all_days = days * lon_count
    depth = inverse_gram.shape[0]
    field = f32(blocks, days, rows, LANES)
    state = (observations, aux_state, dual_state)
    slab = f32(days, rows, columns)
    tile = f32(TILE, columns)
    target, bottom, top = call(
        edges_kernel,
        (slab, tile, tile),
        [IN_HBM] * 3,
        (IN_VMEM,) * 3,
        2.0,
        [pltpu.VMEM((days, 3, rows, columns), jnp.float32), DMA((days, 3))],
        EDGES_MIB,
    )(*state)
    above = lax.ppermute(bottom, "lat", [(i, (i + 1) % lat_count) for i in range(lat_count)])
    below = lax.ppermute(top, "lat", [((i + 1) % lat_count, i) for i in range(lat_count)])
    operator = jnp.asarray(columns_operator(), jnp.bfloat16)
    own = call(functools.partial(own_kernel, lat_count), field, [IN_VMEM] * 2, IN_VMEM, 3.0)(target, operator)
    to_coefficients, to_fitted = call(
        maps_kernel,
        (bf16(depth, 3 * all_days), bf16(all_days, 3 * all_days)),
        [IN_VMEM] * 2,
        (IN_VMEM, IN_VMEM),
        2.0,
    )(predictors, inverse_gram)
    smooth = call(functools.partial(halo_kernel, lat_count), field, [IN_VMEM] * 5, IN_VMEM, 1.5)(
        own, above, below, operator, to_fitted
    )
    smooth = lax.all_to_all(smooth, "lon", 0, 0, tiled=True).reshape(all_days * rows, LANES)
    fitted = call(fitted_kernel, f32(all_days * rows, LANES), [IN_VMEM] * 2, IN_VMEM, 2.0)(smooth, to_fitted)
    fitted = lax.all_to_all(fitted.reshape(field.shape), "lon", 0, 0, tiled=True)
    devices = lat_count * lon_count
    sums = call(sums_kernel, f32(devices, 1, LANES), [IN_VMEM] * 4, IN_VMEM, 1.0)(
        *state, fitted
    )
    coefficients, aux_next, dual_next = call(
        results_kernel,
        (f32(depth * rows, LANES), slab, slab),
        [IN_VMEM] * 5 + [IN_HBM],
        (IN_HBM,) * 3,
        5.0,
        [
            pltpu.VMEM((rows // 2, 3 * all_days, 2 * LANES), jnp.bfloat16),
            pltpu.VMEM((depth * rows, LANES), jnp.float32),
            pltpu.VMEM(slab.shape, jnp.float32),
            pltpu.VMEM(slab.shape, jnp.float32),
            DMA((PARTS + 2 * days,)),
        ],
    )(smooth, to_coefficients, observations, dual_state, fitted, sums)
    coefficients = coefficients.reshape(depth, rows, LANES)
    sums = lax.all_to_all(sums, ("lat", "lon"), 0, 0, tiled=True)
    primal, change = call(norms_kernel, (f32(1, 1), f32(1, 1)), [IN_VMEM], (IN_VMEM, IN_VMEM), 0.5)(sums)
    return (coefficients, aux_next, dual_next, primal.reshape(()), change.reshape(()))


def solution(mesh):
    in_specs = (P("lon", "lat", None), P("lon", "lat", None), P("lon", "lat", None), P(), P())
    out_specs = (P(None, "lat", "lon"), P("lon", "lat", None), P("lon", "lat", None), P(), P())
    body = functools.partial(local, mesh.shape["lat"], mesh.shape["lon"])
    return jax.shard_map(body, mesh=mesh, in_specs=in_specs, out_specs=out_specs, check_vma=False)
```

```python
import functools
import math

import jax
import jax.numpy as jnp
import numpy as np
from jax import lax
from jax.experimental import pallas as pl
from jax.experimental.pallas import tpu as pltpu
from jax.sharding import PartitionSpec as P

SWEEPS = 4
QUANTILE = 0.9
PENALTY = 2.0
SMOOTHING = 1.0
HIGHEST = lax.Precision.HIGHEST
HALO = 4
LANES = 128
TILE = 8
UNROLL = 8
OWN_UNROLL = 32
HALO_UNROLL = 32
PARTS = 8
EDGE_PARTS = 2
EDGES_MIB = 52.5
SCALE = 1.0 / 625.0
IN_VMEM = pl.BlockSpec(memory_space=pltpu.VMEM)
IN_HBM = pl.BlockSpec(memory_space=pltpu.HBM)
DMA = pltpu.SemaphoreType.DMA


def f32(*shape):
    return jax.ShapeDtypeStruct(shape, jnp.float32)


def bf16(*shape):
    return jax.ShapeDtypeStruct(shape, jnp.bfloat16)


def call(kernel, outs, in_specs, out_specs, us, scratch=(), mib=20):
    return pl.pallas_call(
        kernel,
        out_shape=outs,
        in_specs=in_specs,
        out_specs=out_specs,
        scratch_shapes=scratch,
        compiler_params=pltpu.CompilerParams(vmem_limit_bytes=int(mib * 2**20)),
        cost_estimate=pl.CostEstimate(flops=int(us * 1e9), bytes_accessed=0, transcendentals=0),
    )


def iota(shape, dim):
    return lax.broadcasted_iota(jnp.int32, shape, dim)


def columns_operator():
    powers = [np.array([1.0])]
    for _ in range(SWEEPS):
        powers.append(np.convolve(powers[-1], [1.0, 0.0, 1.0]))
    weights = [5.0 ** (SWEEPS - 1 - j) for j in range(SWEEPS)] + [1.0]
    inner = np.zeros((LANES, SWEEPS, LANES))
    outer = np.zeros((LANES, SWEEPS, LANES))
    for k in range(SWEEPS):
        band = np.zeros(2 * SWEEPS + 1)
        for j in range(k, SWEEPS + 1):
            reach = j - k
            band[SWEEPS - reach : SWEEPS + reach + 1] += weights[j] * math.comb(j, k) * powers[reach]
        for lane in range(LANES):
            for step in range(-SWEEPS, SWEEPS + 1):
                source = lane + step
                into = inner if 0 <= source < LANES else outer
                into[source % LANES, k, lane] = band[SWEEPS + step]
    inner, outer = (part.reshape(LANES, SWEEPS * LANES) for part in (inner, outer))
    return np.concatenate([inner, inner, outer, outer], axis=0)


def edges_kernel(obs, aux, dual, target, bottom, top, held, sems):
    days, rows, columns = obs.shape
    part = columns // EDGE_PARTS
    copies = []
    for piece in range(EDGE_PARTS):
        cols = pl.ds(piece * part, part)
        for k, array in enumerate((obs, aux, dual)):
            copies.append(
                pltpu.make_async_copy(array.at[:, :, cols], held.at[k, :, :, cols], sems.at[piece, k])
            )
    for copy in copies:
        copy.start()
    for piece in range(EDGE_PARTS):
        cols = pl.ds(piece * part, part)
        for k in range(3):
            copies[piece * 3 + k].wait()
        target[:, :, cols] = held[0, :, :, cols] - held[1, :, :, cols] + held[2, :, :, cols]
    low = iota(top.shape, 0) < HALO
    last = rows - TILE
    top[...] = jnp.where(low, target[0, :TILE], pltpu.roll(target[1, :TILE], HALO, 0))
    bottom[...] = jnp.where(low, pltpu.roll(target[1, last:], HALO, 0), target[0, last:])


def split(x):
    high = x.astype(jnp.bfloat16)
    return high, (x - high.astype(jnp.float32)).astype(jnp.bfloat16)


def columns_part(blocks, operator):
    first = iota(blocks[0].shape, 1) < LANES // 2
    stacked = []
    for u in range(1, len(blocks) - 1):
        beside = jnp.where(first, blocks[u + 1], blocks[u - 1])
        stacked.append(jnp.concatenate(split(blocks[u]) + split(beside), axis=1))
    return jnp.dot(jnp.concatenate(stacked, axis=0), operator[...], preferred_element_type=jnp.float32)


def own_kernel(lat_count, target, operator, out):
    blocks, days, rows, _ = out.shape
    lat = lax.axis_index("lat")
    total = rows + TILE
    low = iota((TILE, LANES), 0) < HALO
    inside = jnp.where(low, jnp.where(lat < lat_count - 1, 1.0, 0.0), jnp.where(lat > 0, 1.0, 0.0))
    zero = jnp.zeros((TILE, LANES), jnp.float32)

    def body(group, carry):
        start = group * OWN_UNROLL
        held = []
        for u in range(-1, OWN_UNROLL + 1):
            j = lax.rem(start + u + blocks, blocks)
            cols = pl.ds(pl.multiple_of(j * LANES, LANES), LANES)
            held.append(jnp.concatenate([target[day, :, cols] for day in range(days)], axis=0))
        parts = columns_part(held, operator)
        for u in range(OWN_UNROLL):
            for day in range(days):
                at = (u * days + day) * rows
                now = jnp.concatenate([held[u + 1][day * rows : (day + 1) * rows], zero], axis=0)
                for k in reversed(range(SWEEPS)):
                    upright = pltpu.roll(now, 1, 0) + pltpu.roll(now, total - 1, 0)
                    new = upright[:rows] + parts[at : at + rows, k * LANES : (k + 1) * LANES]
                    if k:
                        now = jnp.concatenate([new, upright[rows:] * inside], axis=0)
                out[start + u, day] = new * SCALE
        return carry

    lax.fori_loop(0, blocks // OWN_UNROLL, body, 0)


def halo_kernel(lat_count, own, above, below, operator, after, out):
    blocks, days, rows, _ = own.shape
    row = iota((TILE, LANES), 0)
    low = row < HALO
    begin, end = row == 0, row == TILE - 1
    zero = jnp.zeros((TILE, LANES), jnp.float32)
    lat = lax.axis_index("lat")
    south_scale = jnp.where(lat < lat_count - 1, SCALE, 0.0)
    north_scale = jnp.where(lat > 0, SCALE, 0.0)

    def spread(south, north):
        return (
            (jnp.where(low, pltpu.roll(north, HALO, 0), zero), jnp.where(low, zero, pltpu.roll(south, HALO, 0))),
            (jnp.where(low, north, zero), jnp.where(low, zero, south)),
        )

    def body(group, carry):
        start = group * HALO_UNROLL
        held = []
        for u in range(-1, HALO_UNROLL + 1):
            j = lax.rem(start + u + blocks, blocks)
            cols = pl.ds(pl.multiple_of(j * LANES, LANES), LANES)
            held.append(jnp.concatenate([below[:, cols], above[:, cols]], axis=0))
        parts = columns_part(held, operator)
        for u in range(HALO_UNROLL):
            at = u * 2 * TILE
            now = spread(held[u + 1][:TILE], held[u + 1][TILE:])
            for k in reversed(range(SWEEPS)):
                cols = slice(k * LANES, (k + 1) * LANES)
                part = spread(parts[at : at + TILE, cols], parts[at + TILE : at + 2 * TILE, cols])
                now = tuple(
                    tuple(
                        jnp.where(begin, zero, pltpu.roll(now[day][side], 1, 0))
                        + jnp.where(end, zero, pltpu.roll(now[day][side], TILE - 1, 0))
                        + part[day][side]
                        for side in range(2)
                    )
                    for day in range(days)
                )
            j = start + u
            for day in range(days):
                north = pltpu.roll(now[day][0], HALO, 0) * north_scale
                south = pltpu.roll(now[day][1], HALO, 0) * south_scale
                out[j, day, :TILE] = own[j, day, :TILE] + jnp.where(low, north, zero)
                out[j, day, TILE : rows - TILE] = own[j, day, TILE : rows - TILE]
                out[j, day, rows - TILE :] = own[j, day, rows - TILE :] + jnp.where(low, zero, south)
        return carry

    lax.fori_loop(0, blocks // HALO_UNROLL, body, 0)


def stack_left(matrix):
    high, low = split(matrix)
    return jnp.concatenate([high, low, high], axis=1)


def stack_right(matrix):
    high, low = split(matrix)
    return jnp.concatenate([high, high, low], axis=0)


def maps_kernel(predictors, inverse_gram, to_coefficients, to_fitted):
    scores = predictors[...]
    direct = jnp.dot(stack_left(inverse_gram[...]), stack_right(scores.T), preferred_element_type=jnp.float32)
    back = jnp.dot(stack_left(scores), stack_right(direct), preferred_element_type=jnp.float32)
    to_coefficients[...] = stack_left(direct)
    to_fitted[...] = stack_left(back)


def pairs(smooth, rows, days):
    for r in range(0, rows, 2):
        high, low = split(jnp.concatenate([smooth[pl.ds(r + i, days, stride=rows), :] for i in range(2)], axis=1))
        yield r, jnp.concatenate([high, high, low], axis=0)


def fitted_kernel(smooth, matrix, fitted):
    days = matrix.shape[0]
    rows = smooth.shape[0] // days
    for r, right in pairs(smooth, rows, days):
        both = jnp.dot(matrix[...], right, preferred_element_type=jnp.float32)
        for i in range(2):
            fitted[pl.ds(r + i, days, stride=rows), :] = both[:, i * LANES : (i + 1) * LANES]


def proximal(obs, dual, fitted):
    shifted = obs + dual - fitted
    auxiliary = shifted - jnp.clip(shifted, -(1.0 - QUANTILE) / PENALTY, QUANTILE / PENALTY)
    return auxiliary, shifted - auxiliary


def sums_kernel(obs, aux, dual, fitted, sums):
    blocks, days, rows, _ = fitted.shape

    zero = jnp.zeros((rows, LANES), jnp.float32)
    totals = [[zero, zero] for _ in range(4)]
    for j in range(blocks):
        cols = pl.ds(j * LANES, LANES)
        for day in range(days):
            total = totals[(j * days + day) % len(totals)]
            dual_now = dual[day, :, cols]
            aux_new, dual_new = proximal(obs[day, :, cols], dual_now, fitted[j, day])
            moved = dual_new - dual_now
            total[0] += moved * moved
            moved = aux_new - aux[day, :, cols]
            total[1] += moved * moved
    primal = (totals[0][0] + totals[1][0]) + (totals[2][0] + totals[3][0])
    change = (totals[0][1] + totals[1][1]) + (totals[2][1] + totals[3][1])
    primal = jnp.sum(primal, axis=0, keepdims=True)
    change = jnp.sum(change, axis=0, keepdims=True)
    half = LANES // 2
    both = jnp.where(
        iota((1, LANES), 1) < half, primal + pltpu.roll(primal, half, 1), change + pltpu.roll(change, half, 1)
    )
    sums[...] = jnp.broadcast_to(both, sums.shape)


def results_kernel(
    smooth, matrix, obs, dual, fitted, after, coefficients, aux_next, dual_next, stacked, held, aux_held, dual_held, sems
):
    depth = matrix.shape[0]
    days_all = matrix.shape[1] // 3
    blocks, days, rows, _ = fitted.shape
    part = depth // PARTS
    copies = []

    def send(source, target, k):
        copies.append(pltpu.make_async_copy(source, target, sems.at[k]))
        copies[-1].start(priority=k % 2)

    for r, right in pairs(smooth, rows, days_all):
        stacked[r // 2] = right
    for k in range(PARTS):
        for r in range(0, rows, 2):
            both = jnp.dot(
                matrix[k * part : (k + 1) * part, :], stacked[r // 2], preferred_element_type=jnp.float32
            )
            for i in range(2):
                held[pl.ds(k * part * rows + r + i, part, stride=rows), :] = both[:, i * LANES : (i + 1) * LANES]
        span = pl.ds(k * part * rows, part * rows)
        send(held.at[span], coefficients.at[span], k)

    for day in range(days):

        def body(group, carry):
            for u in range(UNROLL):
                j = group * UNROLL + u
                cols = pl.ds(pl.multiple_of(j * LANES, LANES), LANES)
                aux_new, dual_new = proximal(obs[day, :, cols], dual[day, :, cols], fitted[j, day])
                aux_held[day, :, cols] = aux_new
                dual_held[day, :, cols] = dual_new
            return carry

        lax.fori_loop(0, blocks // UNROLL, body, 0)
        send(aux_held.at[day], aux_next.at[day], PARTS + day)
        send(dual_held.at[day], dual_next.at[day], PARTS + days + day)
    for copy in copies:
        copy.wait()


def norms_kernel(sums, primal, change):
    row = jnp.sum(sums[...], axis=0, keepdims=True)
    half = iota(row.shape, 1) < LANES // 2
    primal[...] = jnp.sqrt(jnp.sum(jnp.where(half, row, 0.0), axis=1, keepdims=True))
    change[...] = PENALTY * jnp.sqrt(jnp.sum(jnp.where(half, 0.0, row), axis=1, keepdims=True))


def local(lat_count, lon_count, observations, aux_state, dual_state, predictors, inverse_gram):
    days, rows, columns = observations.shape
    blocks = columns // LANES
    all_days = days * lon_count
    depth = inverse_gram.shape[0]
    field = f32(blocks, days, rows, LANES)
    state = (observations, aux_state, dual_state)
    slab = f32(days, rows, columns)
    tile = f32(TILE, columns)
    target, bottom, top = call(
        edges_kernel,
        (slab, tile, tile),
        [IN_HBM] * 3,
        (IN_VMEM,) * 3,
        2.0,
        [pltpu.VMEM((3, days, rows, columns), jnp.float32), DMA((EDGE_PARTS, 3))],
        EDGES_MIB,
    )(*state)
    above = lax.ppermute(bottom, "lat", [(i, (i + 1) % lat_count) for i in range(lat_count)])
    below = lax.ppermute(top, "lat", [((i + 1) % lat_count, i) for i in range(lat_count)])
    operator = jnp.asarray(columns_operator(), jnp.bfloat16)
    own = call(functools.partial(own_kernel, lat_count), field, [IN_VMEM] * 2, IN_VMEM, 3.0)(target, operator)
    to_coefficients, to_fitted = call(
        maps_kernel,
        (bf16(depth, 3 * all_days), bf16(all_days, 3 * all_days)),
        [IN_VMEM] * 2,
        (IN_VMEM, IN_VMEM),
        2.0,
    )(predictors, inverse_gram)
    smooth = call(functools.partial(halo_kernel, lat_count), field, [IN_VMEM] * 5, IN_VMEM, 1.5)(
        own, above, below, operator, to_fitted
    )
    smooth = lax.all_to_all(smooth, "lon", 0, 0, tiled=True).reshape(all_days * rows, LANES)
    fitted = call(fitted_kernel, f32(all_days * rows, LANES), [IN_VMEM] * 2, IN_VMEM, 2.0)(smooth, to_fitted)
    fitted = lax.all_to_all(fitted.reshape(field.shape), "lon", 0, 0, tiled=True)
    devices = lat_count * lon_count
    sums = call(sums_kernel, f32(devices, LANES), [IN_VMEM] * 4, IN_VMEM, 1.0)(
        *state, fitted
    )
    coefficients, aux_next, dual_next = call(
        results_kernel,
        (f32(depth * rows, LANES), slab, slab),
        [IN_VMEM] * 5 + [IN_HBM],
        (IN_HBM,) * 3,
        5.0,
        [
            pltpu.VMEM((rows // 2, 3 * all_days, 2 * LANES), jnp.bfloat16),
            pltpu.VMEM((depth * rows, LANES), jnp.float32),
            pltpu.VMEM(slab.shape, jnp.float32),
            pltpu.VMEM(slab.shape, jnp.float32),
            DMA((PARTS + 2 * days,)),
        ],
    )(smooth, to_coefficients, observations, dual_state, fitted, sums)
    coefficients = coefficients.reshape(depth, rows, LANES)
    sums = lax.all_to_all(sums.reshape(devices, 1, LANES), ("lat", "lon"), 0, 0, tiled=True).reshape(devices, LANES)
    primal, change = call(norms_kernel, (f32(1, 1), f32(1, 1)), [IN_VMEM], (IN_VMEM, IN_VMEM), 0.5)(sums)
    return (coefficients, aux_next, dual_next, primal.reshape(()), change.reshape(()))


def solution(mesh):
    in_specs = (P("lon", "lat", None), P("lon", "lat", None), P("lon", "lat", None), P(), P())
    out_specs = (P(None, "lat", "lon"), P("lon", "lat", None), P("lon", "lat", None), P(), P())
    body = functools.partial(local, mesh.shape["lat"], mesh.shape["lon"])
    return jax.shard_map(body, mesh=mesh, in_specs=in_specs, out_specs=out_specs, check_vma=False)
```

```python
import functools
import math

import jax
import jax.numpy as jnp
import numpy as np
from jax import lax
from jax.experimental import pallas as pl
from jax.experimental.pallas import tpu as pltpu
from jax.sharding import PartitionSpec as P

SWEEPS = 4
QUANTILE = 0.9
PENALTY = 2.0
SMOOTHING = 1.0
HIGHEST = lax.Precision.HIGHEST
HALO = 4
LANES = 128
TILE = 8
UNROLL = 8
OWN_UNROLL = 32
PARTS = 8
EDGE_PARTS = 2
EDGES_MIB = 52.5
SCALE = 1.0 / 625.0
IN_VMEM = pl.BlockSpec(memory_space=pltpu.VMEM)
IN_HBM = pl.BlockSpec(memory_space=pltpu.HBM)
DMA = pltpu.SemaphoreType.DMA


def f32(*shape):
    return jax.ShapeDtypeStruct(shape, jnp.float32)


def bf16(*shape):
    return jax.ShapeDtypeStruct(shape, jnp.bfloat16)


def call(kernel, outs, in_specs, out_specs, us, scratch=(), mib=20):
    return pl.pallas_call(
        kernel,
        out_shape=outs,
        in_specs=in_specs,
        out_specs=out_specs,
        scratch_shapes=scratch,
        compiler_params=pltpu.CompilerParams(vmem_limit_bytes=int(mib * 2**20)),
        cost_estimate=pl.CostEstimate(flops=int(us * 1e9), bytes_accessed=0, transcendentals=0),
    )


def iota(shape, dim):
    return lax.broadcasted_iota(jnp.int32, shape, dim)


def columns_bands():
    powers = [np.array([1.0])]
    for _ in range(SWEEPS):
        powers.append(np.convolve(powers[-1], [1.0, 0.0, 1.0]))
    weights = [5.0 ** (SWEEPS - 1 - j) for j in range(SWEEPS)] + [1.0]
    bands = np.zeros((SWEEPS + 1, 2 * SWEEPS + 1))
    for k in range(SWEEPS + 1):
        for j in range(k, SWEEPS + 1):
            reach = j - k
            bands[k, SWEEPS - reach : SWEEPS + reach + 1] += weights[j] * math.comb(j, k) * powers[reach]
    return bands


def distance_bands():
    bands = columns_bands()
    walks = [[math.comb(k, (k + d) // 2) * ((k + d) % 2 == 0) for k in range(SWEEPS + 1)] for d in range(1, SWEEPS)]
    return np.array([sum(walks[d - 1][k] * bands[k] for k in range(d, SWEEPS + 1)) for d in range(1, SWEEPS)])


def columns_operator(bands):
    inner = np.zeros((LANES, len(bands), LANES))
    outer = np.zeros((LANES, len(bands), LANES))
    for k, band in enumerate(bands):
        for lane in range(LANES):
            for step in range(-SWEEPS, SWEEPS + 1):
                source = lane + step
                into = inner if 0 <= source < LANES else outer
                into[source % LANES, k, lane] = band[SWEEPS + step]
    inner, outer = (part.reshape(LANES, len(bands) * LANES) for part in (inner, outer))
    return jnp.asarray(np.concatenate([inner, inner, outer, outer], axis=0), jnp.bfloat16)


def edges_kernel(obs, aux, dual, target, bottom, top, held, sems):
    days, rows, columns = obs.shape
    part = columns // EDGE_PARTS
    copies = []
    for piece in range(EDGE_PARTS):
        cols = pl.ds(piece * part, part)
        for k, array in enumerate((obs, aux, dual)):
            copies.append(
                pltpu.make_async_copy(array.at[:, :, cols], held.at[k, :, :, cols], sems.at[piece, k])
            )
    for copy in copies:
        copy.start()
    for piece in range(EDGE_PARTS):
        cols = pl.ds(piece * part, part)
        for k in range(3):
            copies[piece * 3 + k].wait()
        target[:, :, cols] = held[0, :, :, cols] - held[1, :, :, cols] + held[2, :, :, cols]
    low = iota(top.shape, 0) < HALO
    last = rows - TILE
    top[...] = jnp.where(low, target[0, :TILE], pltpu.roll(target[1, :TILE], HALO, 0))
    bottom[...] = jnp.where(low, pltpu.roll(target[1, last:], HALO, 0), target[0, last:])


def split(x):
    high = x.astype(jnp.bfloat16)
    return high, (x - high.astype(jnp.float32)).astype(jnp.bfloat16)


def columns_part(blocks, operator):
    first = iota(blocks[0].shape, 1) < LANES // 2
    stacked = []
    for u in range(1, len(blocks) - 1):
        beside = jnp.where(first, blocks[u + 1], blocks[u - 1])
        stacked.append(jnp.concatenate(split(blocks[u]) + split(beside), axis=1))
    return jnp.dot(jnp.concatenate(stacked, axis=0), operator[...], preferred_element_type=jnp.float32)


def own_kernel(lat_count, target, operator, out):
    blocks, days, rows, _ = out.shape
    lat = lax.axis_index("lat")
    total = rows + TILE
    low = iota((TILE, LANES), 0) < HALO
    inside = jnp.where(low, jnp.where(lat < lat_count - 1, 1.0, 0.0), jnp.where(lat > 0, 1.0, 0.0))
    zero = jnp.zeros((TILE, LANES), jnp.float32)

    def body(group, carry):
        start = group * OWN_UNROLL
        held = []
        for u in range(-1, OWN_UNROLL + 1):
            j = lax.rem(start + u + blocks, blocks)
            cols = pl.ds(pl.multiple_of(j * LANES, LANES), LANES)
            held.append(jnp.concatenate([target[day, :, cols] for day in range(days)], axis=0))
        parts = columns_part(held, operator)
        for u in range(OWN_UNROLL):
            for day in range(days):
                at = (u * days + day) * rows
                now = jnp.concatenate([held[u + 1][day * rows : (day + 1) * rows], zero], axis=0)
                for k in reversed(range(SWEEPS)):
                    upright = pltpu.roll(now, 1, 0) + pltpu.roll(now, total - 1, 0)
                    new = upright[:rows] + parts[at : at + rows, k * LANES : (k + 1) * LANES]
                    if k:
                        now = jnp.concatenate([new, upright[rows:] * inside], axis=0)
                out[start + u, day] = new * SCALE
        return carry

    lax.fori_loop(0, blocks // OWN_UNROLL, body, 0)


def halo_kernel(lat_count, own, above, below, operator, after, out):
    blocks, days, rows, _ = own.shape
    row = iota((TILE, LANES), 0)
    low = row < HALO
    place = lax.rem(row, HALO)
    zero = jnp.zeros((TILE, LANES), jnp.float32)
    lat = lax.axis_index("lat")
    south_scale = jnp.where(lat < lat_count - 1, SCALE, 0.0)
    north_scale = jnp.where(lat > 0, SCALE, 0.0)
    held = []
    for u in range(-1, blocks + 1):
        cols = pl.ds((u % blocks) * LANES, LANES)
        held.append(jnp.concatenate([below[:, cols], above[:, cols]], axis=0))
    parts = columns_part(held, operator)
    for j in range(blocks):
        at = j * 2 * TILE
        south = pltpu.roll(held[j + 1][:TILE], HALO, 0)
        north = pltpu.roll(held[j + 1][TILE:], HALO, 0)
        for d in range(1, HALO):
            part = parts[at : at + 2 * TILE, (d - 1) * LANES : d * LANES]
            south += jnp.where(place >= HALO - d, pltpu.roll(part[:TILE], TILE - d, 0), zero)
            north += jnp.where(place < d, pltpu.roll(part[TILE:], d, 0), zero)
        south = south * south_scale
        north = north * north_scale
        for day in range(days):
            north_day = north if day == 0 else pltpu.roll(north, HALO, 0)
            south_day = south if day == 0 else pltpu.roll(south, HALO, 0)
            out[j, day, :TILE] = own[j, day, :TILE] + jnp.where(low, north_day, zero)
            out[j, day, TILE : rows - TILE] = own[j, day, TILE : rows - TILE]
            out[j, day, rows - TILE :] = own[j, day, rows - TILE :] + jnp.where(low, zero, south_day)


def stack_left(matrix):
    high, low = split(matrix)
    return jnp.concatenate([high, low, high], axis=1)


def stack_right(matrix):
    high, low = split(matrix)
    return jnp.concatenate([high, high, low], axis=0)


def maps_kernel(predictors, inverse_gram, to_coefficients, to_fitted):
    scores = predictors[...]
    direct = jnp.dot(stack_left(inverse_gram[...]), stack_right(scores.T), preferred_element_type=jnp.float32)
    back = jnp.dot(stack_left(scores), stack_right(direct), preferred_element_type=jnp.float32)
    to_coefficients[...] = stack_left(direct)
    to_fitted[...] = stack_left(back)


def pairs(smooth, rows, days):
    for r in range(0, rows, 2):
        high, low = split(jnp.concatenate([smooth[pl.ds(r + i, days, stride=rows), :] for i in range(2)], axis=1))
        yield r, jnp.concatenate([high, high, low], axis=0)


def fitted_kernel(smooth, matrix, fitted):
    days = matrix.shape[0]
    rows = smooth.shape[0] // days
    for r, right in pairs(smooth, rows, days):
        both = jnp.dot(matrix[...], right, preferred_element_type=jnp.float32)
        for i in range(2):
            fitted[pl.ds(r + i, days, stride=rows), :] = both[:, i * LANES : (i + 1) * LANES]


def proximal(obs, dual, fitted):
    shifted = obs + dual - fitted
    auxiliary = shifted - jnp.clip(shifted, -(1.0 - QUANTILE) / PENALTY, QUANTILE / PENALTY)
    return auxiliary, shifted - auxiliary


def sums_kernel(obs, aux, dual, fitted, sums):
    blocks, days, rows, _ = fitted.shape

    zero = jnp.zeros((rows, LANES), jnp.float32)
    totals = [[zero, zero] for _ in range(4)]
    for j in range(blocks):
        cols = pl.ds(j * LANES, LANES)
        for day in range(days):
            total = totals[(j * days + day) % len(totals)]
            dual_now = dual[day, :, cols]
            aux_new, dual_new = proximal(obs[day, :, cols], dual_now, fitted[j, day])
            moved = dual_new - dual_now
            total[0] += moved * moved
            moved = aux_new - aux[day, :, cols]
            total[1] += moved * moved
    primal = (totals[0][0] + totals[1][0]) + (totals[2][0] + totals[3][0])
    change = (totals[0][1] + totals[1][1]) + (totals[2][1] + totals[3][1])
    primal = jnp.sum(primal, axis=0, keepdims=True)
    change = jnp.sum(change, axis=0, keepdims=True)
    half = LANES // 2
    both = jnp.where(
        iota((1, LANES), 1) < half, primal + pltpu.roll(primal, half, 1), change + pltpu.roll(change, half, 1)
    )
    sums[...] = jnp.broadcast_to(both, sums.shape)


def results_kernel(
    smooth, matrix, obs, dual, fitted, after, coefficients, aux_next, dual_next, stacked, held, aux_held, dual_held, sems
):
    depth = matrix.shape[0]
    days_all = matrix.shape[1] // 3
    blocks, days, rows, _ = fitted.shape
    part = depth // PARTS
    copies = []

    def send(source, target, k):
        copies.append(pltpu.make_async_copy(source, target, sems.at[k]))
        copies[-1].start(priority=k % 2)

    for r, right in pairs(smooth, rows, days_all):
        stacked[r // 2] = right
    for k in range(PARTS):
        for r in range(0, rows, 2):
            both = jnp.dot(
                matrix[k * part : (k + 1) * part, :], stacked[r // 2], preferred_element_type=jnp.float32
            )
            for i in range(2):
                held[pl.ds(k * part * rows + r + i, part, stride=rows), :] = both[:, i * LANES : (i + 1) * LANES]
        span = pl.ds(k * part * rows, part * rows)
        send(held.at[span], coefficients.at[span], k)

    for day in range(days):

        def body(group, carry):
            for u in range(UNROLL):
                j = group * UNROLL + u
                cols = pl.ds(pl.multiple_of(j * LANES, LANES), LANES)
                aux_new, dual_new = proximal(obs[day, :, cols], dual[day, :, cols], fitted[j, day])
                aux_held[day, :, cols] = aux_new
                dual_held[day, :, cols] = dual_new
            return carry

        lax.fori_loop(0, blocks // UNROLL, body, 0)
        send(aux_held.at[day], aux_next.at[day], PARTS + day)
        send(dual_held.at[day], dual_next.at[day], PARTS + days + day)
    for copy in copies:
        copy.wait()


def norms_kernel(sums, primal, change):
    row = jnp.sum(sums[...], axis=0, keepdims=True)
    half = iota(row.shape, 1) < LANES // 2
    primal[...] = jnp.sqrt(jnp.sum(jnp.where(half, row, 0.0), axis=1, keepdims=True))
    change[...] = PENALTY * jnp.sqrt(jnp.sum(jnp.where(half, 0.0, row), axis=1, keepdims=True))


def local(lat_count, lon_count, observations, aux_state, dual_state, predictors, inverse_gram):
    days, rows, columns = observations.shape
    blocks = columns // LANES
    all_days = days * lon_count
    depth = inverse_gram.shape[0]
    field = f32(blocks, days, rows, LANES)
    state = (observations, aux_state, dual_state)
    slab = f32(days, rows, columns)
    tile = f32(TILE, columns)
    target, bottom, top = call(
        edges_kernel,
        (slab, tile, tile),
        [IN_HBM] * 3,
        (IN_VMEM,) * 3,
        2.0,
        [pltpu.VMEM((3, days, rows, columns), jnp.float32), DMA((EDGE_PARTS, 3))],
        EDGES_MIB,
    )(*state)
    above = lax.ppermute(bottom, "lat", [(i, (i + 1) % lat_count) for i in range(lat_count)])
    below = lax.ppermute(top, "lat", [((i + 1) % lat_count, i) for i in range(lat_count)])
    own = call(functools.partial(own_kernel, lat_count), field, [IN_VMEM] * 2, IN_VMEM, 3.0)(
        target, columns_operator(columns_bands()[:SWEEPS])
    )
    to_coefficients, to_fitted = call(
        maps_kernel,
        (bf16(depth, 3 * all_days), bf16(all_days, 3 * all_days)),
        [IN_VMEM] * 2,
        (IN_VMEM, IN_VMEM),
        2.0,
    )(predictors, inverse_gram)
    smooth = call(functools.partial(halo_kernel, lat_count), field, [IN_VMEM] * 5, IN_VMEM, 1.5)(
        own, above, below, columns_operator(distance_bands()), to_fitted
    )
    smooth = lax.all_to_all(smooth, "lon", 0, 0, tiled=True).reshape(all_days * rows, LANES)
    fitted = call(fitted_kernel, f32(all_days * rows, LANES), [IN_VMEM] * 2, IN_VMEM, 2.0)(smooth, to_fitted)
    fitted = lax.all_to_all(fitted.reshape(field.shape), "lon", 0, 0, tiled=True)
    devices = lat_count * lon_count
    sums = call(sums_kernel, f32(devices, LANES), [IN_VMEM] * 4, IN_VMEM, 1.0)(
        *state, fitted
    )
    coefficients, aux_next, dual_next = call(
        results_kernel,
        (f32(depth * rows, LANES), slab, slab),
        [IN_VMEM] * 5 + [IN_HBM],
        (IN_HBM,) * 3,
        5.0,
        [
            pltpu.VMEM((rows // 2, 3 * all_days, 2 * LANES), jnp.bfloat16),
            pltpu.VMEM((depth * rows, LANES), jnp.float32),
            pltpu.VMEM(slab.shape, jnp.float32),
            pltpu.VMEM(slab.shape, jnp.float32),
            DMA((PARTS + 2 * days,)),
        ],
    )(smooth, to_coefficients, observations, dual_state, fitted, sums)
    coefficients = coefficients.reshape(depth, rows, LANES)
    sums = lax.all_to_all(sums.reshape(devices, 1, LANES), ("lat", "lon"), 0, 0, tiled=True).reshape(devices, LANES)
    primal, change = call(norms_kernel, (f32(1, 1), f32(1, 1)), [IN_VMEM], (IN_VMEM, IN_VMEM), 0.5)(sums)
    return (coefficients, aux_next, dual_next, primal.reshape(()), change.reshape(()))


def solution(mesh):
    in_specs = (P("lon", "lat", None), P("lon", "lat", None), P("lon", "lat", None), P(), P())
    out_specs = (P(None, "lat", "lon"), P("lon", "lat", None), P("lon", "lat", None), P(), P())
    body = functools.partial(local, mesh.shape["lat"], mesh.shape["lon"])
    return jax.shard_map(body, mesh=mesh, in_specs=in_specs, out_specs=out_specs, check_vma=False)
```

```python
import functools
import math

import jax
import jax.numpy as jnp
import numpy as np
from jax import lax
from jax.experimental import pallas as pl
from jax.experimental.pallas import tpu as pltpu
from jax.sharding import PartitionSpec as P

SWEEPS = 4
QUANTILE = 0.9
PENALTY = 2.0
SMOOTHING = 1.0
HIGHEST = lax.Precision.HIGHEST
HALO = 4
LANES = 128
TILE = 8
UNROLL = 8
OWN_UNROLL = 32
PARTS = 8
EDGES_MIB = 53.5
SCALE = 1.0 / 625.0
IN_VMEM = pl.BlockSpec(memory_space=pltpu.VMEM)
IN_HBM = pl.BlockSpec(memory_space=pltpu.HBM)
DMA = pltpu.SemaphoreType.DMA


def f32(*shape):
    return jax.ShapeDtypeStruct(shape, jnp.float32)


def bf16(*shape):
    return jax.ShapeDtypeStruct(shape, jnp.bfloat16)


def call(kernel, outs, in_specs, out_specs, us, scratch=(), mib=20):
    return pl.pallas_call(
        kernel,
        out_shape=outs,
        in_specs=in_specs,
        out_specs=out_specs,
        scratch_shapes=scratch,
        compiler_params=pltpu.CompilerParams(vmem_limit_bytes=int(mib * 2**20)),
        cost_estimate=pl.CostEstimate(flops=int(us * 1e9), bytes_accessed=0, transcendentals=0),
    )


def iota(shape, dim):
    return lax.broadcasted_iota(jnp.int32, shape, dim)


def columns_bands():
    powers = [np.array([1.0])]
    for _ in range(SWEEPS):
        powers.append(np.convolve(powers[-1], [1.0, 0.0, 1.0]))
    weights = [5.0 ** (SWEEPS - 1 - j) for j in range(SWEEPS)] + [1.0]
    bands = np.zeros((SWEEPS + 1, 2 * SWEEPS + 1))
    for k in range(SWEEPS + 1):
        for j in range(k, SWEEPS + 1):
            reach = j - k
            bands[k, SWEEPS - reach : SWEEPS + reach + 1] += weights[j] * math.comb(j, k) * powers[reach]
    return bands


def distance_bands():
    bands = columns_bands()
    walks = [[math.comb(k, (k + d) // 2) * ((k + d) % 2 == 0) for k in range(SWEEPS + 1)] for d in range(1, SWEEPS)]
    return np.array([sum(walks[d - 1][k] * bands[k] for k in range(d, SWEEPS + 1)) for d in range(1, SWEEPS)])


def columns_operator(bands):
    inner = np.zeros((LANES, len(bands), LANES))
    outer = np.zeros((LANES, len(bands), LANES))
    for k, band in enumerate(bands):
        for lane in range(LANES):
            for step in range(-SWEEPS, SWEEPS + 1):
                source = lane + step
                into = inner if 0 <= source < LANES else outer
                into[source % LANES, k, lane] = band[SWEEPS + step]
    inner, outer = (part.reshape(LANES, len(bands) * LANES) for part in (inner, outer))
    return jnp.asarray(np.concatenate([inner, inner, outer, outer], axis=0), jnp.bfloat16)


def edges_kernel(obs, aux, dual, bottom, top, held, sems):
    last = obs.shape[1] - TILE
    copies = []
    for side, row in enumerate((0, last)):
        for k, array in enumerate((obs, aux, dual)):
            copies.append(
                pltpu.make_async_copy(array.at[:, pl.ds(row, TILE), :], held.at[side, k], sems.at[side, k])
            )
    for copy in copies:
        copy.start()
    low = iota(top.shape, 0) < HALO

    def target(day, side):
        return held[side, 0, day] - held[side, 1, day] + held[side, 2, day]

    for copy in copies[:3]:
        copy.wait()
    top[...] = jnp.where(low, target(0, 0), pltpu.roll(target(1, 0), HALO, 0))
    for copy in copies[3:]:
        copy.wait()
    bottom[...] = jnp.where(low, pltpu.roll(target(1, 1), HALO, 0), target(0, 1))


def split(x):
    high = x.astype(jnp.bfloat16)
    return high, (x - high.astype(jnp.float32)).astype(jnp.bfloat16)


def columns_part(blocks, operator):
    first = iota(blocks[0].shape, 1) < LANES // 2
    stacked = []
    for u in range(1, len(blocks) - 1):
        beside = jnp.where(first, blocks[u + 1], blocks[u - 1])
        stacked.append(jnp.concatenate(split(blocks[u]) + split(beside), axis=1))
    return jnp.dot(jnp.concatenate(stacked, axis=0), operator[...], preferred_element_type=jnp.float32)


def own_kernel(lat_count, obs, aux, dual, operator, out):
    blocks, days, rows, _ = out.shape
    lat = lax.axis_index("lat")
    total = rows + TILE
    low = iota((TILE, LANES), 0) < HALO
    inside = jnp.where(low, jnp.where(lat < lat_count - 1, 1.0, 0.0), jnp.where(lat > 0, 1.0, 0.0))
    zero = jnp.zeros((TILE, LANES), jnp.float32)

    def body(group, carry):
        start = group * OWN_UNROLL
        held = []
        for u in range(-1, OWN_UNROLL + 1):
            j = lax.rem(start + u + blocks, blocks)
            cols = pl.ds(pl.multiple_of(j * LANES, LANES), LANES)
            target = [obs[day, :, cols] - aux[day, :, cols] + dual[day, :, cols] for day in range(days)]
            held.append(jnp.concatenate(target, axis=0))
        parts = columns_part(held, operator)
        for u in range(OWN_UNROLL):
            for day in range(days):
                at = (u * days + day) * rows
                now = jnp.concatenate([held[u + 1][day * rows : (day + 1) * rows], zero], axis=0)
                for k in reversed(range(SWEEPS)):
                    upright = pltpu.roll(now, 1, 0) + pltpu.roll(now, total - 1, 0)
                    new = upright[:rows] + parts[at : at + rows, k * LANES : (k + 1) * LANES]
                    if k:
                        now = jnp.concatenate([new, upright[rows:] * inside], axis=0)
                out[start + u, day] = new * SCALE
        return carry

    lax.fori_loop(0, blocks // OWN_UNROLL, body, 0)


def halo_kernel(lat_count, own, above, below, operator, after, out):
    blocks, days, rows, _ = own.shape
    row = iota((TILE, LANES), 0)
    low = row < HALO
    place = lax.rem(row, HALO)
    zero = jnp.zeros((TILE, LANES), jnp.float32)
    lat = lax.axis_index("lat")
    south_scale = jnp.where(lat < lat_count - 1, SCALE, 0.0)
    north_scale = jnp.where(lat > 0, SCALE, 0.0)
    held = []
    for u in range(-1, blocks + 1):
        cols = pl.ds((u % blocks) * LANES, LANES)
        held.append(jnp.concatenate([below[:, cols], above[:, cols]], axis=0))
    parts = columns_part(held, operator)
    for j in range(blocks):
        at = j * 2 * TILE
        south = pltpu.roll(held[j + 1][:TILE], HALO, 0)
        north = pltpu.roll(held[j + 1][TILE:], HALO, 0)
        for d in range(1, HALO):
            part = parts[at : at + 2 * TILE, (d - 1) * LANES : d * LANES]
            south += jnp.where(place >= HALO - d, pltpu.roll(part[:TILE], TILE - d, 0), zero)
            north += jnp.where(place < d, pltpu.roll(part[TILE:], d, 0), zero)
        south = south * south_scale
        north = north * north_scale
        for day in range(days):
            north_day = north if day == 0 else pltpu.roll(north, HALO, 0)
            south_day = south if day == 0 else pltpu.roll(south, HALO, 0)
            out[j, day, :TILE] = own[j, day, :TILE] + jnp.where(low, north_day, zero)
            out[j, day, TILE : rows - TILE] = own[j, day, TILE : rows - TILE]
            out[j, day, rows - TILE :] = own[j, day, rows - TILE :] + jnp.where(low, zero, south_day)


def stack_left(matrix):
    high, low = split(matrix)
    return jnp.concatenate([high, low, high], axis=1)


def stack_right(matrix):
    high, low = split(matrix)
    return jnp.concatenate([high, high, low], axis=0)


def maps_kernel(predictors, inverse_gram, to_coefficients, to_fitted):
    scores = predictors[...]
    direct = jnp.dot(stack_left(inverse_gram[...]), stack_right(scores.T), preferred_element_type=jnp.float32)
    back = jnp.dot(stack_left(scores), stack_right(direct), preferred_element_type=jnp.float32)
    to_coefficients[...] = stack_left(direct)
    to_fitted[...] = stack_left(back)


def pairs(smooth, rows, days):
    for r in range(0, rows, 2):
        high, low = split(jnp.concatenate([smooth[pl.ds(r + i, days, stride=rows), :] for i in range(2)], axis=1))
        yield r, jnp.concatenate([high, high, low], axis=0)


def fitted_kernel(smooth, matrix, fitted):
    days = matrix.shape[0]
    rows = smooth.shape[0] // days
    for r, right in pairs(smooth, rows, days):
        both = jnp.dot(matrix[...], right, preferred_element_type=jnp.float32)
        for i in range(2):
            fitted[pl.ds(r + i, days, stride=rows), :] = both[:, i * LANES : (i + 1) * LANES]


def proximal(obs, dual, fitted):
    shifted = obs + dual - fitted
    auxiliary = shifted - jnp.clip(shifted, -(1.0 - QUANTILE) / PENALTY, QUANTILE / PENALTY)
    return auxiliary, shifted - auxiliary


def sums_kernel(obs, aux, dual, fitted, sums):
    blocks, days, rows, _ = fitted.shape

    zero = jnp.zeros((rows, LANES), jnp.float32)
    totals = [[zero, zero] for _ in range(4)]
    for j in range(blocks):
        cols = pl.ds(j * LANES, LANES)
        for day in range(days):
            total = totals[(j * days + day) % len(totals)]
            dual_now = dual[day, :, cols]
            aux_new, dual_new = proximal(obs[day, :, cols], dual_now, fitted[j, day])
            moved = dual_new - dual_now
            total[0] += moved * moved
            moved = aux_new - aux[day, :, cols]
            total[1] += moved * moved
    primal = (totals[0][0] + totals[1][0]) + (totals[2][0] + totals[3][0])
    change = (totals[0][1] + totals[1][1]) + (totals[2][1] + totals[3][1])
    primal = jnp.sum(primal, axis=0, keepdims=True)
    change = jnp.sum(change, axis=0, keepdims=True)
    half = LANES // 2
    both = jnp.where(
        iota((1, LANES), 1) < half, primal + pltpu.roll(primal, half, 1), change + pltpu.roll(change, half, 1)
    )
    sums[...] = jnp.broadcast_to(both, sums.shape)


def results_kernel(
    smooth, matrix, obs, dual, fitted, after, coefficients, aux_next, dual_next, stacked, held, aux_held, dual_held, sems
):
    depth = matrix.shape[0]
    days_all = matrix.shape[1] // 3
    blocks, days, rows, _ = fitted.shape
    part = depth // PARTS
    copies = []

    def send(source, target, k):
        copies.append(pltpu.make_async_copy(source, target, sems.at[k]))
        copies[-1].start(priority=k % 2)

    for r, right in pairs(smooth, rows, days_all):
        stacked[r // 2] = right
    for k in range(PARTS):
        for r in range(0, rows, 2):
            both = jnp.dot(
                matrix[k * part : (k + 1) * part, :], stacked[r // 2], preferred_element_type=jnp.float32
            )
            for i in range(2):
                held[pl.ds(k * part * rows + r + i, part, stride=rows), :] = both[:, i * LANES : (i + 1) * LANES]
        span = pl.ds(k * part * rows, part * rows)
        send(held.at[span], coefficients.at[span], k)

    for day in range(days):

        def body(group, carry):
            for u in range(UNROLL):
                j = group * UNROLL + u
                cols = pl.ds(pl.multiple_of(j * LANES, LANES), LANES)
                aux_new, dual_new = proximal(obs[day, :, cols], dual[day, :, cols], fitted[j, day])
                aux_held[day, :, cols] = aux_new
                dual_held[day, :, cols] = dual_new
            return carry

        lax.fori_loop(0, blocks // UNROLL, body, 0)
        send(aux_held.at[day], aux_next.at[day], PARTS + day)
        send(dual_held.at[day], dual_next.at[day], PARTS + days + day)
    for copy in copies:
        copy.wait()


def norms_kernel(sums, primal, change):
    row = jnp.sum(sums[...], axis=0, keepdims=True)
    half = iota(row.shape, 1) < LANES // 2
    primal[...] = jnp.sqrt(jnp.sum(jnp.where(half, row, 0.0), axis=1, keepdims=True))
    change[...] = PENALTY * jnp.sqrt(jnp.sum(jnp.where(half, 0.0, row), axis=1, keepdims=True))


def local(lat_count, lon_count, observations, aux_state, dual_state, predictors, inverse_gram):
    days, rows, columns = observations.shape
    blocks = columns // LANES
    all_days = days * lon_count
    depth = inverse_gram.shape[0]
    field = f32(blocks, days, rows, LANES)
    state = (observations, aux_state, dual_state)
    slab = f32(days, rows, columns)
    tile = f32(TILE, columns)
    bottom, top = call(
        edges_kernel,
        (tile, tile),
        [IN_HBM] * 3,
        (IN_VMEM,) * 2,
        2.0,
        [pltpu.VMEM((2, 3, days, TILE, columns), jnp.float32), DMA((2, 3))],
        EDGES_MIB,
    )(*state)
    above = lax.ppermute(bottom, "lat", [(i, (i + 1) % lat_count) for i in range(lat_count)])
    below = lax.ppermute(top, "lat", [((i + 1) % lat_count, i) for i in range(lat_count)])
    own = call(functools.partial(own_kernel, lat_count), field, [IN_VMEM] * 4, IN_VMEM, 3.0)(
        *state, columns_operator(columns_bands()[:SWEEPS])
    )
    to_coefficients, to_fitted = call(
        maps_kernel,
        (bf16(depth, 3 * all_days), bf16(all_days, 3 * all_days)),
        [IN_VMEM] * 2,
        (IN_VMEM, IN_VMEM),
        2.0,
    )(predictors, inverse_gram)
    smooth = call(functools.partial(halo_kernel, lat_count), field, [IN_VMEM] * 5, IN_VMEM, 1.5)(
        own, above, below, columns_operator(distance_bands()), to_fitted
    )
    smooth = lax.all_to_all(smooth, "lon", 0, 0, tiled=True).reshape(all_days * rows, LANES)
    fitted = call(fitted_kernel, f32(all_days * rows, LANES), [IN_VMEM] * 2, IN_VMEM, 2.0)(smooth, to_fitted)
    fitted = lax.all_to_all(fitted.reshape(field.shape), "lon", 0, 0, tiled=True)
    devices = lat_count * lon_count
    sums = call(sums_kernel, f32(devices, LANES), [IN_VMEM] * 4, IN_VMEM, 1.0)(
        *state, fitted
    )
    coefficients, aux_next, dual_next = call(
        results_kernel,
        (f32(depth * rows, LANES), slab, slab),
        [IN_VMEM] * 5 + [IN_HBM],
        (IN_HBM,) * 3,
        5.0,
        [
            pltpu.VMEM((rows // 2, 3 * all_days, 2 * LANES), jnp.bfloat16),
            pltpu.VMEM((depth * rows, LANES), jnp.float32),
            pltpu.VMEM(slab.shape, jnp.float32),
            pltpu.VMEM(slab.shape, jnp.float32),
            DMA((PARTS + 2 * days,)),
        ],
    )(smooth, to_coefficients, observations, dual_state, fitted, sums)
    coefficients = coefficients.reshape(depth, rows, LANES)
    sums = lax.all_to_all(sums.reshape(devices, 1, LANES), ("lat", "lon"), 0, 0, tiled=True).reshape(devices, LANES)
    primal, change = call(norms_kernel, (f32(1, 1), f32(1, 1)), [IN_VMEM], (IN_VMEM, IN_VMEM), 0.5)(sums)
    return (coefficients, aux_next, dual_next, primal.reshape(()), change.reshape(()))


def solution(mesh):
    in_specs = (P("lon", "lat", None), P("lon", "lat", None), P("lon", "lat", None), P(), P())
    out_specs = (P(None, "lat", "lon"), P("lon", "lat", None), P("lon", "lat", None), P(), P())
    body = functools.partial(local, mesh.shape["lat"], mesh.shape["lon"])
    return jax.shard_map(body, mesh=mesh, in_specs=in_specs, out_specs=out_specs, check_vma=False)
```

```python
import functools
import math

import jax
import jax.numpy as jnp
import numpy as np
from jax import lax
from jax.experimental import pallas as pl
from jax.experimental.pallas import tpu as pltpu
from jax.sharding import PartitionSpec as P

SWEEPS = 4
QUANTILE = 0.9
PENALTY = 2.0
SMOOTHING = 1.0
HIGHEST = lax.Precision.HIGHEST
HALO = 4
LANES = 128
TILE = 8
UNROLL = 8
OWN_UNROLL = 32
PARTS = 8
EDGES_MIB = 53.5
SCALE = 1.0 / 625.0
IN_VMEM = pl.BlockSpec(memory_space=pltpu.VMEM)
IN_HBM = pl.BlockSpec(memory_space=pltpu.HBM)
DMA = pltpu.SemaphoreType.DMA


def f32(*shape):
    return jax.ShapeDtypeStruct(shape, jnp.float32)


def bf16(*shape):
    return jax.ShapeDtypeStruct(shape, jnp.bfloat16)


def call(kernel, outs, in_specs, out_specs, us, scratch=(), mib=20):
    return pl.pallas_call(
        kernel,
        out_shape=outs,
        in_specs=in_specs,
        out_specs=out_specs,
        scratch_shapes=scratch,
        compiler_params=pltpu.CompilerParams(vmem_limit_bytes=int(mib * 2**20)),
        cost_estimate=pl.CostEstimate(flops=int(us * 1e9), bytes_accessed=0, transcendentals=0),
    )


def iota(shape, dim):
    return lax.broadcasted_iota(jnp.int32, shape, dim)


def columns_bands():
    powers = [np.array([1.0])]
    for _ in range(SWEEPS):
        powers.append(np.convolve(powers[-1], [1.0, 0.0, 1.0]))
    weights = [5.0 ** (SWEEPS - 1 - j) for j in range(SWEEPS)] + [1.0]
    bands = np.zeros((SWEEPS + 1, 2 * SWEEPS + 1))
    for k in range(SWEEPS + 1):
        for j in range(k, SWEEPS + 1):
            reach = j - k
            bands[k, SWEEPS - reach : SWEEPS + reach + 1] += weights[j] * math.comb(j, k) * powers[reach]
    return bands


def distance_bands():
    bands = columns_bands()
    walks = [[math.comb(k, (k + d) // 2) * ((k + d) % 2 == 0) for k in range(SWEEPS + 1)] for d in range(1, SWEEPS)]
    return np.array([sum(walks[d - 1][k] * bands[k] for k in range(d, SWEEPS + 1)) for d in range(1, SWEEPS)])


def columns_operator(bands):
    inner = np.zeros((LANES, len(bands), LANES))
    outer = np.zeros((LANES, len(bands), LANES))
    for k, band in enumerate(bands):
        for lane in range(LANES):
            for step in range(-SWEEPS, SWEEPS + 1):
                source = lane + step
                into = inner if 0 <= source < LANES else outer
                into[source % LANES, k, lane] = band[SWEEPS + step]
    inner, outer = (part.reshape(LANES, len(bands) * LANES) for part in (inner, outer))
    return jnp.asarray(np.concatenate([inner, inner, outer, outer], axis=0), jnp.bfloat16)


def edges_kernel(obs, aux, dual, first, second, held, sems):
    last = obs.shape[1] - TILE
    copies = []
    for side, row in enumerate((0, last)):
        for k, array in enumerate((obs, aux, dual)):
            copies.append(
                pltpu.make_async_copy(array.at[:, pl.ds(row, TILE), :], held.at[side, k], sems.at[side, k])
            )
    for copy in copies:
        copy.start()
    low = iota(first.shape, 0) < HALO
    even = lax.rem(lax.axis_index("lat"), 2) == 0

    def target(day, side):
        return held[side, 0, day] - held[side, 1, day] + held[side, 2, day]

    for copy in copies[:3]:
        copy.wait()
    top = jnp.where(low, target(0, 0), pltpu.roll(target(1, 0), HALO, 0))
    for copy in copies[3:]:
        copy.wait()
    bottom = jnp.where(low, pltpu.roll(target(1, 1), HALO, 0), target(0, 1))
    first[...] = jnp.where(even, bottom, top)
    second[...] = jnp.where(even, top, bottom)


def split(x):
    high = x.astype(jnp.bfloat16)
    return high, (x - high.astype(jnp.float32)).astype(jnp.bfloat16)


def columns_part(blocks, operator):
    first = iota(blocks[0].shape, 1) < LANES // 2
    stacked = []
    for u in range(1, len(blocks) - 1):
        beside = jnp.where(first, blocks[u + 1], blocks[u - 1])
        stacked.append(jnp.concatenate(split(blocks[u]) + split(beside), axis=1))
    return jnp.dot(jnp.concatenate(stacked, axis=0), operator[...], preferred_element_type=jnp.float32)


def own_kernel(lat_count, obs, aux, dual, operator, out):
    blocks, days, rows, _ = out.shape
    lat = lax.axis_index("lat")
    total = rows + TILE
    low = iota((TILE, LANES), 0) < HALO
    inside = jnp.where(low, jnp.where(lat < lat_count - 1, 1.0, 0.0), jnp.where(lat > 0, 1.0, 0.0))
    zero = jnp.zeros((TILE, LANES), jnp.float32)

    def body(group, carry):
        start = group * OWN_UNROLL
        held = []
        for u in range(-1, OWN_UNROLL + 1):
            j = lax.rem(start + u + blocks, blocks)
            cols = pl.ds(pl.multiple_of(j * LANES, LANES), LANES)
            target = [obs[day, :, cols] - aux[day, :, cols] + dual[day, :, cols] for day in range(days)]
            held.append(jnp.concatenate(target, axis=0))
        parts = columns_part(held, operator)
        for u in range(OWN_UNROLL):
            for day in range(days):
                at = (u * days + day) * rows
                now = jnp.concatenate([held[u + 1][day * rows : (day + 1) * rows], zero], axis=0)
                for k in reversed(range(SWEEPS)):
                    upright = pltpu.roll(now, 1, 0) + pltpu.roll(now, total - 1, 0)
                    new = upright[:rows] + parts[at : at + rows, k * LANES : (k + 1) * LANES]
                    if k:
                        now = jnp.concatenate([new, upright[rows:] * inside], axis=0)
                out[start + u, day] = new * SCALE
        return carry

    lax.fori_loop(0, blocks // OWN_UNROLL, body, 0)


def halo_kernel(lat_count, own, second, first, operator, after, out):
    blocks, days, rows, _ = own.shape
    row = iota((TILE, LANES), 0)
    low = row < HALO
    place = lax.rem(row, HALO)
    zero = jnp.zeros((TILE, LANES), jnp.float32)
    lat = lax.axis_index("lat")
    even = lax.rem(lat, 2) == 0
    south_scale = jnp.where(lat < lat_count - 1, SCALE, 0.0)
    north_scale = jnp.where(lat > 0, SCALE, 0.0)
    held = []
    for u in range(-1, blocks + 1):
        cols = pl.ds((u % blocks) * LANES, LANES)
        one, two = first[:, cols], second[:, cols]
        held.append(jnp.concatenate([jnp.where(even, one, two), jnp.where(even, two, one)], axis=0))
    parts = columns_part(held, operator)
    for j in range(blocks):
        at = j * 2 * TILE
        south = pltpu.roll(held[j + 1][:TILE], HALO, 0)
        north = pltpu.roll(held[j + 1][TILE:], HALO, 0)
        for d in range(1, HALO):
            part = parts[at : at + 2 * TILE, (d - 1) * LANES : d * LANES]
            south += jnp.where(place >= HALO - d, pltpu.roll(part[:TILE], TILE - d, 0), zero)
            north += jnp.where(place < d, pltpu.roll(part[TILE:], d, 0), zero)
        south = south * south_scale
        north = north * north_scale
        for day in range(days):
            north_day = north if day == 0 else pltpu.roll(north, HALO, 0)
            south_day = south if day == 0 else pltpu.roll(south, HALO, 0)
            out[j, day, :TILE] = own[j, day, :TILE] + jnp.where(low, north_day, zero)
            out[j, day, TILE : rows - TILE] = own[j, day, TILE : rows - TILE]
            out[j, day, rows - TILE :] = own[j, day, rows - TILE :] + jnp.where(low, zero, south_day)


def stack_left(matrix):
    high, low = split(matrix)
    return jnp.concatenate([high, low, high], axis=1)


def maps_kernel(predictors, inverse_gram, to_coefficients, to_fitted):
    scores = predictors[...]
    contract = (((1,), (1,)), ((), ()))
    direct = lax.dot_general(
        inverse_gram[...], scores, contract, precision=HIGHEST, preferred_element_type=jnp.float32
    )
    back = jnp.dot(scores, direct, precision=HIGHEST, preferred_element_type=jnp.float32)
    to_coefficients[...] = stack_left(direct)
    to_fitted[...] = stack_left(back)


def pairs(smooth, rows, days):
    for r in range(0, rows, 2):
        high, low = split(jnp.concatenate([smooth[pl.ds(r + i, days, stride=rows), :] for i in range(2)], axis=1))
        yield r, jnp.concatenate([high, high, low], axis=0)


def fitted_kernel(smooth, matrix, fitted):
    days = matrix.shape[0]
    rows = smooth.shape[0] // days
    for r, right in pairs(smooth, rows, days):
        both = jnp.dot(matrix[...], right, preferred_element_type=jnp.float32)
        for i in range(2):
            fitted[pl.ds(r + i, days, stride=rows), :] = both[:, i * LANES : (i + 1) * LANES]


def proximal(obs, dual, fitted):
    shifted = obs + dual - fitted
    auxiliary = shifted - jnp.clip(shifted, -(1.0 - QUANTILE) / PENALTY, QUANTILE / PENALTY)
    return auxiliary, shifted - auxiliary


def sums_kernel(obs, aux, dual, fitted, sums):
    blocks, days, rows, _ = fitted.shape

    zero = jnp.zeros((rows, LANES), jnp.float32)
    totals = [[zero, zero] for _ in range(4)]
    for j in range(blocks):
        cols = pl.ds(j * LANES, LANES)
        for day in range(days):
            total = totals[(j * days + day) % len(totals)]
            dual_now = dual[day, :, cols]
            aux_new, dual_new = proximal(obs[day, :, cols], dual_now, fitted[j, day])
            moved = dual_new - dual_now
            total[0] += moved * moved
            moved = aux_new - aux[day, :, cols]
            total[1] += moved * moved
    primal = (totals[0][0] + totals[1][0]) + (totals[2][0] + totals[3][0])
    change = (totals[0][1] + totals[1][1]) + (totals[2][1] + totals[3][1])
    primal = jnp.sum(primal, axis=0, keepdims=True)
    change = jnp.sum(change, axis=0, keepdims=True)
    half = LANES // 2
    both = jnp.where(
        iota((1, LANES), 1) < half, primal + pltpu.roll(primal, half, 1), change + pltpu.roll(change, half, 1)
    )
    sums[...] = jnp.broadcast_to(both, sums.shape)


def results_kernel(
    smooth, matrix, obs, dual, fitted, after, coefficients, aux_next, dual_next, stacked, held, aux_held, dual_held, sems
):
    depth = matrix.shape[0]
    days_all = matrix.shape[1] // 3
    blocks, days, rows, _ = fitted.shape
    part = depth // PARTS
    copies = []

    def send(source, target, k):
        copies.append(pltpu.make_async_copy(source, target, sems.at[k]))
        copies[-1].start(priority=k % 2)

    for day in range(days):

        def body(group, carry):
            for u in range(UNROLL):
                j = group * UNROLL + u
                cols = pl.ds(pl.multiple_of(j * LANES, LANES), LANES)
                aux_new, dual_new = proximal(obs[day, :, cols], dual[day, :, cols], fitted[j, day])
                aux_held[day, :, cols] = aux_new
                dual_held[day, :, cols] = dual_new
            return carry

        lax.fori_loop(0, blocks // UNROLL, body, 0)
        send(aux_held.at[day], aux_next.at[day], PARTS + day)
        send(dual_held.at[day], dual_next.at[day], PARTS + days + day)

    for r, right in pairs(smooth, rows, days_all):
        stacked[r // 2] = right
    for k in range(PARTS):
        for r in range(0, rows, 2):
            both = jnp.dot(
                matrix[k * part : (k + 1) * part, :], stacked[r // 2], preferred_element_type=jnp.float32
            )
            for i in range(2):
                held[pl.ds(k * part * rows + r + i, part, stride=rows), :] = both[:, i * LANES : (i + 1) * LANES]
        span = pl.ds(k * part * rows, part * rows)
        send(held.at[span], coefficients.at[span], k)
    for copy in copies:
        copy.wait()


def norms_kernel(sums, primal, change):
    row = jnp.sum(sums[...], axis=0, keepdims=True)
    half = iota(row.shape, 1) < LANES // 2
    primal[...] = jnp.sqrt(jnp.sum(jnp.where(half, row, 0.0), axis=1, keepdims=True))
    change[...] = PENALTY * jnp.sqrt(jnp.sum(jnp.where(half, 0.0, row), axis=1, keepdims=True))


def local(lat_count, lon_count, observations, aux_state, dual_state, predictors, inverse_gram):
    days, rows, columns = observations.shape
    blocks = columns // LANES
    all_days = days * lon_count
    depth = inverse_gram.shape[0]
    field = f32(blocks, days, rows, LANES)
    state = (observations, aux_state, dual_state)
    slab = f32(days, rows, columns)
    tile = f32(TILE, columns)
    first, second = call(
        edges_kernel,
        (tile, tile),
        [IN_HBM] * 3,
        (IN_VMEM,) * 2,
        2.0,
        [pltpu.VMEM((2, 3, days, TILE, columns), jnp.float32), DMA((2, 3))],
        EDGES_MIB,
    )(*state)
    first = lax.ppermute(first, "lat", [(i, i ^ 1) for i in range(lat_count)])
    second = lax.ppermute(second, "lat", [(i, i ^ 3) for i in range(lat_count)])
    own = call(functools.partial(own_kernel, lat_count), field, [IN_VMEM] * 4, IN_VMEM, 3.0)(
        *state, columns_operator(columns_bands()[:SWEEPS])
    )
    to_coefficients, to_fitted = call(
        maps_kernel,
        (bf16(depth, 3 * all_days), bf16(all_days, 3 * all_days)),
        [IN_VMEM] * 2,
        (IN_VMEM, IN_VMEM),
        2.0,
    )(predictors, inverse_gram)
    smooth = call(functools.partial(halo_kernel, lat_count), field, [IN_VMEM] * 5, IN_VMEM, 1.5)(
        own, second, first, columns_operator(distance_bands()), to_fitted
    )
    smooth = lax.all_to_all(smooth, "lon", 0, 0, tiled=True).reshape(all_days * rows, LANES)
    fitted = call(fitted_kernel, f32(all_days * rows, LANES), [IN_VMEM] * 2, IN_VMEM, 2.0)(smooth, to_fitted)
    fitted = lax.all_to_all(fitted.reshape(field.shape), "lon", 0, 0, tiled=True)
    devices = lat_count * lon_count
    sums = call(sums_kernel, f32(devices, LANES), [IN_VMEM] * 4, IN_VMEM, 1.0)(
        *state, fitted
    )
    coefficients, aux_next, dual_next = call(
        results_kernel,
        (f32(depth * rows, LANES), slab, slab),
        [IN_VMEM] * 5 + [IN_HBM],
        (IN_HBM,) * 3,
        5.0,
        [
            pltpu.VMEM((rows // 2, 3 * all_days, 2 * LANES), jnp.bfloat16),
            pltpu.VMEM((depth * rows, LANES), jnp.float32),
            pltpu.VMEM(slab.shape, jnp.float32),
            pltpu.VMEM(slab.shape, jnp.float32),
            DMA((PARTS + 2 * days,)),
        ],
    )(smooth, to_coefficients, observations, dual_state, fitted, sums)
    coefficients = coefficients.reshape(depth, rows, LANES)
    sums = lax.all_to_all(sums.reshape(devices, 1, LANES), ("lat", "lon"), 0, 0, tiled=True).reshape(devices, LANES)
    primal, change = call(norms_kernel, (f32(1, 1), f32(1, 1)), [IN_VMEM], (IN_VMEM, IN_VMEM), 0.5)(sums)
    return (coefficients, aux_next, dual_next, primal.reshape(()), change.reshape(()))


def solution(mesh):
    in_specs = (P("lon", "lat", None), P("lon", "lat", None), P("lon", "lat", None), P(), P())
    out_specs = (P(None, "lat", "lon"), P("lon", "lat", None), P("lon", "lat", None), P(), P())
    body = functools.partial(local, mesh.shape["lat"], mesh.shape["lon"])
    return jax.shard_map(body, mesh=mesh, in_specs=in_specs, out_specs=out_specs, check_vma=False)
```

```python
import functools
import math

import jax
import jax.numpy as jnp
import numpy as np
from jax import lax
from jax.experimental import pallas as pl
from jax.experimental.pallas import tpu as pltpu
from jax.sharding import PartitionSpec as P

SWEEPS = 4
QUANTILE = 0.9
PENALTY = 2.0
SMOOTHING = 1.0
HIGHEST = lax.Precision.HIGHEST
HALO = 4
LANES = 128
TILE = 8
UNROLL = 8
OWN_UNROLL = 32
PARTS = 8
EDGES_MIB = 53.5
SCALE = 1.0 / 625.0
IN_VMEM = pl.BlockSpec(memory_space=pltpu.VMEM)
IN_HBM = pl.BlockSpec(memory_space=pltpu.HBM)
DMA = pltpu.SemaphoreType.DMA


def middle_pairs(lat_count, lon_count):
    pairs = []
    for lat in range(lat_count):
        for lon in range(lon_count):
            other = (lat + 1 if lat % 2 else lat - 1, lon)
            if not 0 <= other[0] < lat_count:
                other = (lat, lon ^ 1)
            pairs.append((lat * lon_count + lon, other[0] * lon_count + other[1]))
    return pairs


def f32(*shape):
    return jax.ShapeDtypeStruct(shape, jnp.float32)


def bf16(*shape):
    return jax.ShapeDtypeStruct(shape, jnp.bfloat16)


def call(kernel, outs, in_specs, out_specs, us, scratch=(), mib=20):
    return pl.pallas_call(
        kernel,
        out_shape=outs,
        in_specs=in_specs,
        out_specs=out_specs,
        scratch_shapes=scratch,
        compiler_params=pltpu.CompilerParams(vmem_limit_bytes=int(mib * 2**20)),
        cost_estimate=pl.CostEstimate(flops=int(us * 1e9), bytes_accessed=0, transcendentals=0),
    )


def iota(shape, dim):
    return lax.broadcasted_iota(jnp.int32, shape, dim)


def columns_bands():
    powers = [np.array([1.0])]
    for _ in range(SWEEPS):
        powers.append(np.convolve(powers[-1], [1.0, 0.0, 1.0]))
    weights = [5.0 ** (SWEEPS - 1 - j) for j in range(SWEEPS)] + [1.0]
    bands = np.zeros((SWEEPS + 1, 2 * SWEEPS + 1))
    for k in range(SWEEPS + 1):
        for j in range(k, SWEEPS + 1):
            reach = j - k
            bands[k, SWEEPS - reach : SWEEPS + reach + 1] += weights[j] * math.comb(j, k) * powers[reach]
    return bands


def distance_bands():
    bands = columns_bands()
    walks = [[math.comb(k, (k + d) // 2) * ((k + d) % 2 == 0) for k in range(SWEEPS + 1)] for d in range(1, SWEEPS)]
    return np.array([sum(walks[d - 1][k] * bands[k] for k in range(d, SWEEPS + 1)) for d in range(1, SWEEPS)])


def columns_operator(bands):
    inner = np.zeros((LANES, len(bands), LANES))
    outer = np.zeros((LANES, len(bands), LANES))
    for k, band in enumerate(bands):
        for lane in range(LANES):
            for step in range(-SWEEPS, SWEEPS + 1):
                source = lane + step
                into = inner if 0 <= source < LANES else outer
                into[source % LANES, k, lane] = band[SWEEPS + step]
    inner, outer = (part.reshape(LANES, len(bands) * LANES) for part in (inner, outer))
    return jnp.asarray(np.concatenate([inner, inner, outer, outer], axis=0), jnp.bfloat16)


def edges_kernel(obs, aux, dual, first, second, held, sems):
    last = obs.shape[1] - TILE
    copies = []
    for side, row in enumerate((0, last)):
        for k, array in enumerate((obs, aux, dual)):
            copies.append(
                pltpu.make_async_copy(array.at[:, pl.ds(row, TILE), :], held.at[side, k], sems.at[side, k])
            )
    for copy in copies:
        copy.start()
    low = iota(first.shape, 0) < HALO
    even = lax.rem(lax.axis_index("lat"), 2) == 0

    def target(day, side):
        return held[side, 0, day] - held[side, 1, day] + held[side, 2, day]

    for copy in copies[:3]:
        copy.wait()
    top = jnp.where(low, target(0, 0), pltpu.roll(target(1, 0), HALO, 0))
    for copy in copies[3:]:
        copy.wait()
    bottom = jnp.where(low, pltpu.roll(target(1, 1), HALO, 0), target(0, 1))
    first[...] = jnp.where(even, bottom, top)
    second[...] = jnp.where(even, top, bottom)


def split(x):
    high = x.astype(jnp.bfloat16)
    return high, (x - high.astype(jnp.float32)).astype(jnp.bfloat16)


def columns_part(blocks, operator):
    first = iota(blocks[0].shape, 1) < LANES // 2
    stacked = []
    for u in range(1, len(blocks) - 1):
        beside = jnp.where(first, blocks[u + 1], blocks[u - 1])
        stacked.append(jnp.concatenate(split(blocks[u]) + split(beside), axis=1))
    return jnp.dot(jnp.concatenate(stacked, axis=0), operator[...], preferred_element_type=jnp.float32)


def own_kernel(lat_count, obs, aux, dual, operator, out):
    blocks, days, rows, _ = out.shape
    lat = lax.axis_index("lat")
    total = rows + TILE
    low = iota((TILE, LANES), 0) < HALO
    inside = jnp.where(low, jnp.where(lat < lat_count - 1, 1.0, 0.0), jnp.where(lat > 0, 1.0, 0.0))
    zero = jnp.zeros((TILE, LANES), jnp.float32)

    def body(group, carry):
        start = group * OWN_UNROLL
        held = []
        for u in range(-1, OWN_UNROLL + 1):
            j = lax.rem(start + u + blocks, blocks)
            cols = pl.ds(pl.multiple_of(j * LANES, LANES), LANES)
            target = [obs[day, :, cols] - aux[day, :, cols] + dual[day, :, cols] for day in range(days)]
            held.append(jnp.concatenate(target, axis=0))
        parts = columns_part(held, operator)
        for u in range(OWN_UNROLL):
            for day in range(days):
                at = (u * days + day) * rows
                now = jnp.concatenate([held[u + 1][day * rows : (day + 1) * rows], zero], axis=0)
                for k in reversed(range(SWEEPS)):
                    upright = pltpu.roll(now, 1, 0) + pltpu.roll(now, total - 1, 0)
                    new = upright[:rows] + parts[at : at + rows, k * LANES : (k + 1) * LANES]
                    if k:
                        now = jnp.concatenate([new, upright[rows:] * inside], axis=0)
                out[start + u, day] = new * SCALE
        return carry

    lax.fori_loop(0, blocks // OWN_UNROLL, body, 0)


def halo_kernel(lat_count, own, second, first, operator, after, out):
    blocks, days, rows, _ = own.shape
    row = iota((TILE, LANES), 0)
    low = row < HALO
    place = lax.rem(row, HALO)
    zero = jnp.zeros((TILE, LANES), jnp.float32)
    lat = lax.axis_index("lat")
    even = lax.rem(lat, 2) == 0
    south_scale = jnp.where(lat < lat_count - 1, SCALE, 0.0)
    north_scale = jnp.where(lat > 0, SCALE, 0.0)
    held = []
    for u in range(-1, blocks + 1):
        cols = pl.ds((u % blocks) * LANES, LANES)
        one, two = first[:, cols], second[:, cols]
        held.append(jnp.concatenate([jnp.where(even, one, two), jnp.where(even, two, one)], axis=0))
    parts = columns_part(held, operator)
    for j in range(blocks):
        at = j * 2 * TILE
        south = pltpu.roll(held[j + 1][:TILE], HALO, 0)
        north = pltpu.roll(held[j + 1][TILE:], HALO, 0)
        for d in range(1, HALO):
            part = parts[at : at + 2 * TILE, (d - 1) * LANES : d * LANES]
            south += jnp.where(place >= HALO - d, pltpu.roll(part[:TILE], TILE - d, 0), zero)
            north += jnp.where(place < d, pltpu.roll(part[TILE:], d, 0), zero)
        south = south * south_scale
        north = north * north_scale
        for day in range(days):
            north_day = north if day == 0 else pltpu.roll(north, HALO, 0)
            south_day = south if day == 0 else pltpu.roll(south, HALO, 0)
            out[j, day, :TILE] = own[j, day, :TILE] + jnp.where(low, north_day, zero)
            out[j, day, TILE : rows - TILE] = own[j, day, TILE : rows - TILE]
            out[j, day, rows - TILE :] = own[j, day, rows - TILE :] + jnp.where(low, zero, south_day)


def stack_left(matrix):
    high, low = split(matrix)
    return jnp.concatenate([high, low, high], axis=1)


def maps_kernel(predictors, inverse_gram, to_coefficients, to_fitted):
    scores = predictors[...]
    contract = (((1,), (1,)), ((), ()))
    direct = lax.dot_general(
        inverse_gram[...], scores, contract, precision=HIGHEST, preferred_element_type=jnp.float32
    )
    back = jnp.dot(scores, direct, precision=HIGHEST, preferred_element_type=jnp.float32)
    to_coefficients[...] = stack_left(direct)
    to_fitted[...] = stack_left(back)


def pairs(smooth, rows, days):
    for r in range(0, rows, 2):
        high, low = split(jnp.concatenate([smooth[pl.ds(r + i, days, stride=rows), :] for i in range(2)], axis=1))
        yield r, jnp.concatenate([high, high, low], axis=0)


def fitted_kernel(smooth, matrix, fitted):
    days = matrix.shape[0]
    rows = smooth.shape[0] // days
    for r, right in pairs(smooth, rows, days):
        both = jnp.dot(matrix[...], right, preferred_element_type=jnp.float32)
        for i in range(2):
            fitted[pl.ds(r + i, days, stride=rows), :] = both[:, i * LANES : (i + 1) * LANES]


def proximal(obs, dual, fitted):
    shifted = obs + dual - fitted
    auxiliary = shifted - jnp.clip(shifted, -(1.0 - QUANTILE) / PENALTY, QUANTILE / PENALTY)
    return auxiliary, shifted - auxiliary


def sums_kernel(obs, aux, dual, fitted, sums):
    blocks, days, rows, _ = fitted.shape

    zero = jnp.zeros((rows, LANES), jnp.float32)
    totals = [[zero, zero] for _ in range(4)]
    for j in range(blocks):
        cols = pl.ds(j * LANES, LANES)
        for day in range(days):
            total = totals[(j * days + day) % len(totals)]
            dual_now = dual[day, :, cols]
            aux_new, dual_new = proximal(obs[day, :, cols], dual_now, fitted[j, day])
            moved = dual_new - dual_now
            total[0] += moved * moved
            moved = aux_new - aux[day, :, cols]
            total[1] += moved * moved
    primal = (totals[0][0] + totals[1][0]) + (totals[2][0] + totals[3][0])
    change = (totals[0][1] + totals[1][1]) + (totals[2][1] + totals[3][1])
    primal = jnp.sum(primal, axis=0, keepdims=True)
    change = jnp.sum(change, axis=0, keepdims=True)
    half = LANES // 2
    both = jnp.where(
        iota((1, LANES), 1) < half, primal + pltpu.roll(primal, half, 1), change + pltpu.roll(change, half, 1)
    )
    sums[...] = jnp.broadcast_to(both, sums.shape)


def results_kernel(
    smooth, matrix, obs, dual, fitted, after, coefficients, aux_next, dual_next, stacked, held, aux_held, dual_held, sems
):
    depth = matrix.shape[0]
    days_all = matrix.shape[1] // 3
    blocks, days, rows, _ = fitted.shape
    part = depth // PARTS
    copies = []

    def send(source, target, k):
        copies.append(pltpu.make_async_copy(source, target, sems.at[k]))
        copies[-1].start(priority=k % 2)

    for day in range(days):

        def body(group, carry):
            for u in range(UNROLL):
                j = group * UNROLL + u
                cols = pl.ds(pl.multiple_of(j * LANES, LANES), LANES)
                aux_new, dual_new = proximal(obs[day, :, cols], dual[day, :, cols], fitted[j, day])
                aux_held[day, :, cols] = aux_new
                dual_held[day, :, cols] = dual_new
            return carry

        lax.fori_loop(0, blocks // UNROLL, body, 0)
        send(aux_held.at[day], aux_next.at[day], PARTS + day)
        send(dual_held.at[day], dual_next.at[day], PARTS + days + day)

    for r, right in pairs(smooth, rows, days_all):
        stacked[r // 2] = right
    for k in range(PARTS):
        for r in range(0, rows, 2):
            both = jnp.dot(
                matrix[k * part : (k + 1) * part, :], stacked[r // 2], preferred_element_type=jnp.float32
            )
            for i in range(2):
                held[pl.ds(k * part * rows + r + i, part, stride=rows), :] = both[:, i * LANES : (i + 1) * LANES]
        span = pl.ds(k * part * rows, part * rows)
        send(held.at[span], coefficients.at[span], k)
    for copy in copies:
        copy.wait()


def norms_kernel(sums, primal, change):
    row = jnp.sum(sums[...], axis=0, keepdims=True)
    half = iota(row.shape, 1) < LANES // 2
    primal[...] = jnp.sqrt(jnp.sum(jnp.where(half, row, 0.0), axis=1, keepdims=True))
    change[...] = PENALTY * jnp.sqrt(jnp.sum(jnp.where(half, 0.0, row), axis=1, keepdims=True))


def local(lat_count, lon_count, observations, aux_state, dual_state, predictors, inverse_gram):
    days, rows, columns = observations.shape
    blocks = columns // LANES
    all_days = days * lon_count
    depth = inverse_gram.shape[0]
    field = f32(blocks, days, rows, LANES)
    state = (observations, aux_state, dual_state)
    slab = f32(days, rows, columns)
    tile = f32(TILE, columns)
    first, second = call(
        edges_kernel,
        (tile, tile),
        [IN_HBM] * 3,
        (IN_VMEM,) * 2,
        2.0,
        [pltpu.VMEM((2, 3, days, TILE, columns), jnp.float32), DMA((2, 3))],
        EDGES_MIB,
    )(*state)
    first = lax.ppermute(first, "lat", [(i, i ^ 1) for i in range(lat_count)])
    second = lax.ppermute(second, ("lat", "lon"), middle_pairs(lat_count, lon_count))
    own = call(functools.partial(own_kernel, lat_count), field, [IN_VMEM] * 4, IN_VMEM, 3.0)(
        *state, columns_operator(columns_bands()[:SWEEPS])
    )
    to_coefficients, to_fitted = call(
        maps_kernel,
        (bf16(depth, 3 * all_days), bf16(all_days, 3 * all_days)),
        [IN_VMEM] * 2,
        (IN_VMEM, IN_VMEM),
        2.0,
    )(predictors, inverse_gram)
    smooth = call(functools.partial(halo_kernel, lat_count), field, [IN_VMEM] * 5, IN_VMEM, 1.5)(
        own, second, first, columns_operator(distance_bands()), to_fitted
    )
    smooth = lax.all_to_all(smooth, "lon", 0, 0, tiled=True).reshape(all_days * rows, LANES)
    fitted = call(fitted_kernel, f32(all_days * rows, LANES), [IN_VMEM] * 2, IN_VMEM, 2.0)(smooth, to_fitted)
    fitted = lax.all_to_all(fitted.reshape(field.shape), "lon", 0, 0, tiled=True)
    devices = lat_count * lon_count
    sums = call(sums_kernel, f32(devices, LANES), [IN_VMEM] * 4, IN_VMEM, 1.0)(
        *state, fitted
    )
    coefficients, aux_next, dual_next = call(
        results_kernel,
        (f32(depth * rows, LANES), slab, slab),
        [IN_VMEM] * 5 + [IN_HBM],
        (IN_HBM,) * 3,
        5.0,
        [
            pltpu.VMEM((rows // 2, 3 * all_days, 2 * LANES), jnp.bfloat16),
            pltpu.VMEM((depth * rows, LANES), jnp.float32),
            pltpu.VMEM(slab.shape, jnp.float32),
            pltpu.VMEM(slab.shape, jnp.float32),
            DMA((PARTS + 2 * days,)),
        ],
    )(smooth, to_coefficients, observations, dual_state, fitted, sums)
    coefficients = coefficients.reshape(depth, rows, LANES)
    sums = lax.all_to_all(sums.reshape(devices, 1, LANES), ("lat", "lon"), 0, 0, tiled=True).reshape(devices, LANES)
    primal, change = call(norms_kernel, (f32(1, 1), f32(1, 1)), [IN_VMEM], (IN_VMEM, IN_VMEM), 0.5)(sums)
    return (coefficients, aux_next, dual_next, primal.reshape(()), change.reshape(()))


def solution(mesh):
    in_specs = (P("lon", "lat", None), P("lon", "lat", None), P("lon", "lat", None), P(), P())
    out_specs = (P(None, "lat", "lon"), P("lon", "lat", None), P("lon", "lat", None), P(), P())
    body = functools.partial(local, mesh.shape["lat"], mesh.shape["lon"])
    return jax.shard_map(body, mesh=mesh, in_specs=in_specs, out_specs=out_specs, check_vma=False)
```

```python
import functools
import math

import jax
import jax.numpy as jnp
import numpy as np
from jax import lax
from jax.experimental import pallas as pl
from jax.experimental.pallas import tpu as pltpu
from jax.sharding import PartitionSpec as P

SWEEPS = 4
QUANTILE = 0.9
PENALTY = 2.0
SMOOTHING = 1.0
HIGHEST = lax.Precision.HIGHEST
HALO = 4
LANES = 128
TILE = 8
UNROLL = 8
OWN_UNROLL = 32
PARTS = 8
EDGES_MIB = 53.5
SCALE = 1.0 / 625.0
IN_VMEM = pl.BlockSpec(memory_space=pltpu.VMEM)
IN_HBM = pl.BlockSpec(memory_space=pltpu.HBM)
DMA = pltpu.SemaphoreType.DMA


def middle_pairs(lat_count, lon_count):
    pairs = []
    for lat in range(lat_count):
        for lon in range(lon_count):
            other = (lat + 1 if lat % 2 else lat - 1, lon)
            if not 0 <= other[0] < lat_count:
                other = (lat, lon ^ 1)
            pairs.append((lat * lon_count + lon, other[0] * lon_count + other[1]))
    return pairs


def f32(*shape):
    return jax.ShapeDtypeStruct(shape, jnp.float32)


def bf16(*shape):
    return jax.ShapeDtypeStruct(shape, jnp.bfloat16)


def call(kernel, outs, in_specs, out_specs, us, scratch=(), mib=20):
    return pl.pallas_call(
        kernel,
        out_shape=outs,
        in_specs=in_specs,
        out_specs=out_specs,
        scratch_shapes=scratch,
        compiler_params=pltpu.CompilerParams(vmem_limit_bytes=int(mib * 2**20)),
        cost_estimate=pl.CostEstimate(flops=int(us * 1e9), bytes_accessed=0, transcendentals=0),
    )


def iota(shape, dim):
    return lax.broadcasted_iota(jnp.int32, shape, dim)


def columns_bands():
    powers = [np.array([1.0])]
    for _ in range(SWEEPS):
        powers.append(np.convolve(powers[-1], [1.0, 0.0, 1.0]))
    weights = [5.0 ** (SWEEPS - 1 - j) for j in range(SWEEPS)] + [1.0]
    bands = np.zeros((SWEEPS + 1, 2 * SWEEPS + 1))
    for k in range(SWEEPS + 1):
        for j in range(k, SWEEPS + 1):
            reach = j - k
            bands[k, SWEEPS - reach : SWEEPS + reach + 1] += weights[j] * math.comb(j, k) * powers[reach]
    return bands


def distance_bands():
    bands = columns_bands()
    walks = [[math.comb(k, (k + d) // 2) * ((k + d) % 2 == 0) for k in range(SWEEPS + 1)] for d in range(1, SWEEPS)]
    return np.array([sum(walks[d - 1][k] * bands[k] for k in range(d, SWEEPS + 1)) for d in range(1, SWEEPS)])


def columns_operator(bands):
    inner = np.zeros((LANES, len(bands), LANES))
    outer = np.zeros((LANES, len(bands), LANES))
    for k, band in enumerate(bands):
        for lane in range(LANES):
            for step in range(-SWEEPS, SWEEPS + 1):
                source = lane + step
                into = inner if 0 <= source < LANES else outer
                into[source % LANES, k, lane] = band[SWEEPS + step]
    inner, outer = (part.reshape(LANES, len(bands) * LANES) for part in (inner, outer))
    return jnp.asarray(np.concatenate([inner, inner, outer, outer], axis=0), jnp.bfloat16)


def edges_kernel(obs, aux, dual, first, second, held, sems):
    last = obs.shape[1] - TILE
    copies = []
    for side, row in enumerate((0, last)):
        for k, array in enumerate((obs, aux, dual)):
            copies.append(
                pltpu.make_async_copy(array.at[:, pl.ds(row, TILE), :], held.at[side, k], sems.at[side, k])
            )
    for copy in copies:
        copy.start()
    low = iota(first.shape, 0) < HALO
    even = lax.rem(lax.axis_index("lat"), 2) == 0

    def target(day, side):
        return held[side, 0, day] - held[side, 1, day] + held[side, 2, day]

    for copy in copies[:3]:
        copy.wait()
    top = jnp.where(low, target(0, 0), pltpu.roll(target(1, 0), HALO, 0))
    for copy in copies[3:]:
        copy.wait()
    bottom = jnp.where(low, pltpu.roll(target(1, 1), HALO, 0), target(0, 1))
    first[...] = jnp.where(even, bottom, top)
    second[...] = jnp.where(even, top, bottom)


def split(x):
    high = x.astype(jnp.bfloat16)
    return high, (x - high.astype(jnp.float32)).astype(jnp.bfloat16)


def columns_part(blocks, operator):
    first = iota(blocks[0].shape, 1) < LANES // 2
    stacked = []
    for u in range(1, len(blocks) - 1):
        beside = jnp.where(first, blocks[u + 1], blocks[u - 1])
        stacked.append(jnp.concatenate(split(blocks[u]) + split(beside), axis=1))
    return jnp.dot(jnp.concatenate(stacked, axis=0), operator[...], preferred_element_type=jnp.float32)


def own_kernel(lat_count, obs, aux, dual, operator, out):
    blocks, days, rows, _ = out.shape
    lat = lax.axis_index("lat")
    total = rows + TILE
    low = iota((TILE, LANES), 0) < HALO
    inside = jnp.where(low, jnp.where(lat < lat_count - 1, 1.0, 0.0), jnp.where(lat > 0, 1.0, 0.0))
    zero = jnp.zeros((TILE, LANES), jnp.float32)

    def body(group, carry):
        start = group * OWN_UNROLL
        held = []
        for u in range(-1, OWN_UNROLL + 1):
            j = lax.rem(start + u + blocks, blocks)
            cols = pl.ds(pl.multiple_of(j * LANES, LANES), LANES)
            target = [obs[day, :, cols] - aux[day, :, cols] + dual[day, :, cols] for day in range(days)]
            held.append(jnp.concatenate(target, axis=0))
        parts = columns_part(held, operator)
        for u in range(OWN_UNROLL):
            for day in range(days):
                at = (u * days + day) * rows
                now = jnp.concatenate([held[u + 1][day * rows : (day + 1) * rows], zero], axis=0)
                for k in reversed(range(SWEEPS)):
                    upright = pltpu.roll(now, 1, 0) + pltpu.roll(now, total - 1, 0)
                    new = upright[:rows] + parts[at : at + rows, k * LANES : (k + 1) * LANES]
                    if k:
                        now = jnp.concatenate([new, upright[rows:] * inside], axis=0)
                out[start + u, day] = new * SCALE
        return carry

    lax.fori_loop(0, blocks // OWN_UNROLL, body, 0)


def halo_kernel(lat_count, own, second, first, operator, after, out):
    blocks, days, rows, _ = own.shape
    row = iota((TILE, LANES), 0)
    low = row < HALO
    place = lax.rem(row, HALO)
    zero = jnp.zeros((TILE, LANES), jnp.float32)
    lat = lax.axis_index("lat")
    even = lax.rem(lat, 2) == 0
    south_scale = jnp.where(lat < lat_count - 1, SCALE, 0.0)
    north_scale = jnp.where(lat > 0, SCALE, 0.0)
    held = []
    for u in range(-1, blocks + 1):
        cols = pl.ds((u % blocks) * LANES, LANES)
        one, two = first[:, cols], second[:, cols]
        held.append(jnp.concatenate([jnp.where(even, one, two), jnp.where(even, two, one)], axis=0))
    parts = columns_part(held, operator)
    for j in range(blocks):
        at = j * 2 * TILE
        south = pltpu.roll(held[j + 1][:TILE], HALO, 0)
        north = pltpu.roll(held[j + 1][TILE:], HALO, 0)
        for d in range(1, HALO):
            part = parts[at : at + 2 * TILE, (d - 1) * LANES : d * LANES]
            south += jnp.where(place >= HALO - d, pltpu.roll(part[:TILE], TILE - d, 0), zero)
            north += jnp.where(place < d, pltpu.roll(part[TILE:], d, 0), zero)
        south = south * south_scale
        north = north * north_scale
        for day in range(days):
            north_day = north if day == 0 else pltpu.roll(north, HALO, 0)
            south_day = south if day == 0 else pltpu.roll(south, HALO, 0)
            out[j, day, :TILE] = own[j, day, :TILE] + jnp.where(low, north_day, zero)
            out[j, day, TILE : rows - TILE] = own[j, day, TILE : rows - TILE]
            out[j, day, rows - TILE :] = own[j, day, rows - TILE :] + jnp.where(low, zero, south_day)


def stack_left(matrix):
    high, low = split(matrix)
    return jnp.concatenate([high, low, high], axis=1)


def maps_kernel(predictors, inverse_gram, to_coefficients, to_fitted):
    scores = predictors[...]
    contract = (((1,), (1,)), ((), ()))
    direct = lax.dot_general(
        inverse_gram[...], scores, contract, precision=HIGHEST, preferred_element_type=jnp.float32
    )
    back = jnp.dot(scores, direct, precision=HIGHEST, preferred_element_type=jnp.float32)
    to_coefficients[...] = stack_left(direct)
    to_fitted[...] = stack_left(back)


def pairs(smooth, rows, days):
    for r in range(0, rows, 2):
        high, low = split(jnp.concatenate([smooth[pl.ds(r + i, days, stride=rows), :] for i in range(2)], axis=1))
        yield r, jnp.concatenate([high, high, low], axis=0)


def fitted_kernel(smooth, matrix, fitted):
    days = matrix.shape[0]
    rows = smooth.shape[0] // days
    for r, right in pairs(smooth, rows, days):
        both = jnp.dot(matrix[...], right, preferred_element_type=jnp.float32)
        for i in range(2):
            fitted[pl.ds(r + i, days, stride=rows), :] = both[:, i * LANES : (i + 1) * LANES]


def proximal(obs, dual, fitted):
    shifted = obs + dual - fitted
    auxiliary = shifted - jnp.clip(shifted, -(1.0 - QUANTILE) / PENALTY, QUANTILE / PENALTY)
    return auxiliary, shifted - auxiliary


def sums_kernel(obs, aux, dual, fitted, sums):
    blocks, days, rows, _ = fitted.shape

    zero = jnp.zeros((rows, LANES), jnp.float32)
    totals = [[zero, zero] for _ in range(4)]
    for j in range(blocks):
        cols = pl.ds(j * LANES, LANES)
        for day in range(days):
            total = totals[(j * days + day) % len(totals)]
            dual_now = dual[day, :, cols]
            aux_new, dual_new = proximal(obs[day, :, cols], dual_now, fitted[j, day])
            moved = dual_new - dual_now
            total[0] += moved * moved
            moved = aux_new - aux[day, :, cols]
            total[1] += moved * moved
    primal = (totals[0][0] + totals[1][0]) + (totals[2][0] + totals[3][0])
    change = (totals[0][1] + totals[1][1]) + (totals[2][1] + totals[3][1])
    primal = jnp.sum(primal, axis=0, keepdims=True)
    change = jnp.sum(change, axis=0, keepdims=True)
    half = LANES // 2
    both = jnp.where(
        iota((1, LANES), 1) < half, primal + pltpu.roll(primal, half, 1), change + pltpu.roll(change, half, 1)
    )
    sums[...] = jnp.broadcast_to(both, sums.shape)


def results_kernel(
    smooth, matrix, obs, dual, fitted, after, coefficients, aux_next, dual_next, stacked, held, aux_held, dual_held, sems
):
    depth = matrix.shape[0]
    days_all = matrix.shape[1] // 3
    blocks, days, rows, _ = fitted.shape
    part = depth // PARTS
    copies = []

    def send(source, target, k):
        copies.append(pltpu.make_async_copy(source, target, sems.at[k]))
        copies[-1].start(priority=k % 2)

    for day in range(days):

        def body(group, carry):
            for u in range(UNROLL):
                j = group * UNROLL + u
                cols = pl.ds(pl.multiple_of(j * LANES, LANES), LANES)
                aux_new, dual_new = proximal(obs[day, :, cols], dual[day, :, cols], fitted[j, day])
                aux_held[day, :, cols] = aux_new
                dual_held[day, :, cols] = dual_new
            return carry

        lax.fori_loop(0, blocks // UNROLL, body, 0)
        send(aux_held.at[day], aux_next.at[day], PARTS + day)
        send(dual_held.at[day], dual_next.at[day], PARTS + days + day)

    for r, right in pairs(smooth, rows, days_all):
        stacked[r // 2] = right
    for k in range(PARTS):
        for r in range(0, rows, 2):
            both = jnp.dot(
                matrix[k * part : (k + 1) * part, :], stacked[r // 2], preferred_element_type=jnp.float32
            )
            for i in range(2):
                held[pl.ds(k * part * rows + r + i, part, stride=rows), :] = both[:, i * LANES : (i + 1) * LANES]
        span = pl.ds(k * part * rows, part * rows)
        send(held.at[span], coefficients.at[span], k)
    for copy in copies:
        copy.wait()


def norms_kernel(sums, primal, change):
    row = jnp.sum(sums[...], axis=0, keepdims=True)
    half = (iota((TILE, LANES), 1) < LANES // 2) == (iota((TILE, LANES), 0) == 0)
    norms = jnp.sqrt(jnp.sum(jnp.where(half, row, 0.0), axis=1, keepdims=True))
    primal[...] = norms[:1]
    change[...] = PENALTY * norms[1:2]


def local(lat_count, lon_count, observations, aux_state, dual_state, predictors, inverse_gram):
    days, rows, columns = observations.shape
    blocks = columns // LANES
    all_days = days * lon_count
    depth = inverse_gram.shape[0]
    field = f32(blocks, days, rows, LANES)
    state = (observations, aux_state, dual_state)
    slab = f32(days, rows, columns)
    tile = f32(TILE, columns)
    first, second = call(
        edges_kernel,
        (tile, tile),
        [IN_HBM] * 3,
        (IN_VMEM,) * 2,
        2.0,
        [pltpu.VMEM((2, 3, days, TILE, columns), jnp.float32), DMA((2, 3))],
        EDGES_MIB,
    )(*state)
    first = lax.ppermute(first, "lat", [(i, i ^ 1) for i in range(lat_count)])
    second = lax.ppermute(second, ("lat", "lon"), middle_pairs(lat_count, lon_count))
    own = call(functools.partial(own_kernel, lat_count), field, [IN_VMEM] * 4, IN_VMEM, 3.0)(
        *state, columns_operator(columns_bands()[:SWEEPS])
    )
    to_coefficients, to_fitted = call(
        maps_kernel,
        (bf16(depth, 3 * all_days), bf16(all_days, 3 * all_days)),
        [IN_VMEM] * 2,
        (IN_VMEM, IN_VMEM),
        2.0,
    )(predictors, inverse_gram)
    smooth = call(functools.partial(halo_kernel, lat_count), field, [IN_VMEM] * 5, IN_VMEM, 1.5)(
        own, second, first, columns_operator(distance_bands()), to_fitted
    )
    smooth = lax.all_to_all(smooth, "lon", 0, 0, tiled=True).reshape(all_days * rows, LANES)
    fitted = call(fitted_kernel, f32(all_days * rows, LANES), [IN_VMEM] * 2, IN_VMEM, 2.0)(smooth, to_fitted)
    fitted = lax.all_to_all(fitted.reshape(field.shape), "lon", 0, 0, tiled=True)
    devices = lat_count * lon_count
    sums = call(sums_kernel, f32(devices, LANES), [IN_VMEM] * 4, IN_VMEM, 1.0)(
        *state, fitted
    )
    coefficients, aux_next, dual_next = call(
        results_kernel,
        (f32(depth * rows, LANES), slab, slab),
        [IN_VMEM] * 5 + [IN_HBM],
        (IN_HBM,) * 3,
        5.0,
        [
            pltpu.VMEM((rows // 2, 3 * all_days, 2 * LANES), jnp.bfloat16),
            pltpu.VMEM((depth * rows, LANES), jnp.float32),
            pltpu.VMEM(slab.shape, jnp.float32),
            pltpu.VMEM(slab.shape, jnp.float32),
            DMA((PARTS + 2 * days,)),
        ],
    )(smooth, to_coefficients, observations, dual_state, fitted, sums)
    coefficients = coefficients.reshape(depth, rows, LANES)
    sums = lax.all_to_all(sums.reshape(devices, 1, LANES), ("lat", "lon"), 0, 0, tiled=True).reshape(devices, LANES)
    primal, change = call(norms_kernel, (f32(1, 1), f32(1, 1)), [IN_VMEM], (IN_VMEM, IN_VMEM), 0.5)(sums)
    return (coefficients, aux_next, dual_next, primal.reshape(()), change.reshape(()))


def solution(mesh):
    in_specs = (P("lon", "lat", None), P("lon", "lat", None), P("lon", "lat", None), P(), P())
    out_specs = (P(None, "lat", "lon"), P("lon", "lat", None), P("lon", "lat", None), P(), P())
    body = functools.partial(local, mesh.shape["lat"], mesh.shape["lon"])
    return jax.shard_map(body, mesh=mesh, in_specs=in_specs, out_specs=out_specs, check_vma=False)
```

```python
import functools
import math

import jax
import jax.numpy as jnp
import numpy as np
from jax import lax
from jax.experimental import pallas as pl
from jax.experimental.pallas import tpu as pltpu
from jax.sharding import PartitionSpec as P

SWEEPS = 4
QUANTILE = 0.9
PENALTY = 2.0
SMOOTHING = 1.0
HIGHEST = lax.Precision.HIGHEST
HALO = 4
LANES = 128
TILE = 8
UNROLL = 8
OWN_UNROLL = 32
PARTS = 8
EDGES_MIB = 53.5
SCALE = 1.0 / 625.0
IN_VMEM = pl.BlockSpec(memory_space=pltpu.VMEM)
IN_HBM = pl.BlockSpec(memory_space=pltpu.HBM)
DMA = pltpu.SemaphoreType.DMA


def middle_pairs(lat_count, lon_count):
    pairs = []
    for lat in range(lat_count):
        for lon in range(lon_count):
            other = (lat + 1 if lat % 2 else lat - 1, lon)
            if not 0 <= other[0] < lat_count:
                other = (lat, lon ^ 1)
            pairs.append((lat * lon_count + lon, other[0] * lon_count + other[1]))
    return pairs


def f32(*shape):
    return jax.ShapeDtypeStruct(shape, jnp.float32)


def bf16(*shape):
    return jax.ShapeDtypeStruct(shape, jnp.bfloat16)


def call(kernel, outs, in_specs, out_specs, us, scratch=(), mib=20):
    return pl.pallas_call(
        kernel,
        out_shape=outs,
        in_specs=in_specs,
        out_specs=out_specs,
        scratch_shapes=scratch,
        compiler_params=pltpu.CompilerParams(vmem_limit_bytes=int(mib * 2**20)),
        cost_estimate=pl.CostEstimate(flops=int(us * 1e9), bytes_accessed=0, transcendentals=0),
    )


def iota(shape, dim):
    return lax.broadcasted_iota(jnp.int32, shape, dim)


def columns_bands():
    powers = [np.array([1.0])]
    for _ in range(SWEEPS):
        powers.append(np.convolve(powers[-1], [1.0, 0.0, 1.0]))
    weights = [5.0 ** (SWEEPS - 1 - j) for j in range(SWEEPS)] + [1.0]
    bands = np.zeros((SWEEPS + 1, 2 * SWEEPS + 1))
    for k in range(SWEEPS + 1):
        for j in range(k, SWEEPS + 1):
            reach = j - k
            bands[k, SWEEPS - reach : SWEEPS + reach + 1] += weights[j] * math.comb(j, k) * powers[reach]
    return bands


def distance_bands():
    bands = columns_bands()
    walks = [[math.comb(k, (k + d) // 2) * ((k + d) % 2 == 0) for k in range(SWEEPS + 1)] for d in range(1, SWEEPS)]
    return np.array([sum(walks[d - 1][k] * bands[k] for k in range(d, SWEEPS + 1)) for d in range(1, SWEEPS)])


def columns_operator(bands):
    inner = np.zeros((LANES, len(bands), LANES))
    outer = np.zeros((LANES, len(bands), LANES))
    for k, band in enumerate(bands):
        for lane in range(LANES):
            for step in range(-SWEEPS, SWEEPS + 1):
                source = lane + step
                into = inner if 0 <= source < LANES else outer
                into[source % LANES, k, lane] = band[SWEEPS + step]
    inner, outer = (part.reshape(LANES, len(bands) * LANES) for part in (inner, outer))
    return jnp.asarray(np.concatenate([inner, inner, outer, outer], axis=0), jnp.bfloat16)


def edges_kernel(obs, aux, dual, first, second, held, sems):
    last = obs.shape[1] - TILE
    copies = []
    for side, row in enumerate((0, last)):
        for k, array in enumerate((obs, aux, dual)):
            copies.append(
                pltpu.make_async_copy(array.at[:, pl.ds(row, TILE), :], held.at[side, k], sems.at[side, k])
            )
    for copy in copies:
        copy.start()
    low = iota(first.shape, 0) < HALO
    even = lax.rem(lax.axis_index("lat"), 2) == 0

    def target(day, side):
        return held[side, 0, day] - held[side, 1, day] + held[side, 2, day]

    for copy in copies[:3]:
        copy.wait()
    top = jnp.where(low, target(0, 0), pltpu.roll(target(1, 0), HALO, 0))
    for copy in copies[3:]:
        copy.wait()
    bottom = jnp.where(low, pltpu.roll(target(1, 1), HALO, 0), target(0, 1))
    first[...] = jnp.where(even, bottom, top)
    second[...] = jnp.where(even, top, bottom)


def split(x):
    high = x.astype(jnp.bfloat16)
    return high, (x - high.astype(jnp.float32)).astype(jnp.bfloat16)


def columns_part(blocks, operator):
    first = iota(blocks[0].shape, 1) < LANES // 2
    stacked = []
    for u in range(1, len(blocks) - 1):
        beside = jnp.where(first, blocks[u + 1], blocks[u - 1])
        stacked.append(jnp.concatenate(split(blocks[u]) + split(beside), axis=1))
    return jnp.dot(jnp.concatenate(stacked, axis=0), operator[...], preferred_element_type=jnp.float32)


def own_kernel(lat_count, obs, aux, dual, operator, out):
    blocks, days, rows, _ = out.shape
    lat = lax.axis_index("lat")
    total = rows + TILE
    low = iota((TILE, LANES), 0) < HALO
    inside = jnp.where(low, jnp.where(lat < lat_count - 1, 1.0, 0.0), jnp.where(lat > 0, 1.0, 0.0))
    zero = jnp.zeros((TILE, LANES), jnp.float32)

    def body(group, carry):
        start = group * OWN_UNROLL
        held = []
        for u in range(-1, OWN_UNROLL + 1):
            j = lax.rem(start + u + blocks, blocks)
            cols = pl.ds(pl.multiple_of(j * LANES, LANES), LANES)
            target = [obs[day, :, cols] - aux[day, :, cols] + dual[day, :, cols] for day in range(days)]
            held.append(jnp.concatenate(target, axis=0))
        parts = columns_part(held, operator)
        for u in range(OWN_UNROLL):
            for day in range(days):
                at = (u * days + day) * rows
                now = jnp.concatenate([held[u + 1][day * rows : (day + 1) * rows], zero], axis=0)
                for k in reversed(range(SWEEPS)):
                    upright = pltpu.roll(now, 1, 0) + pltpu.roll(now, total - 1, 0)
                    new = upright[:rows] + parts[at : at + rows, k * LANES : (k + 1) * LANES]
                    if k:
                        now = jnp.concatenate([new, upright[rows:] * inside], axis=0)
                out[start + u, day] = new * SCALE
        return carry

    lax.fori_loop(0, blocks // OWN_UNROLL, body, 0)


def halo_kernel(lat_count, own, second, first, operator, after, out):
    blocks, days, rows, _ = own.shape
    row = iota((TILE, LANES), 0)
    low = row < HALO
    place = lax.rem(row, HALO)
    zero = jnp.zeros((TILE, LANES), jnp.float32)
    lat = lax.axis_index("lat")
    even = lax.rem(lat, 2) == 0
    south_scale = jnp.where(lat < lat_count - 1, SCALE, 0.0)
    north_scale = jnp.where(lat > 0, SCALE, 0.0)
    held = []
    for u in range(-1, blocks + 1):
        cols = pl.ds((u % blocks) * LANES, LANES)
        one, two = first[:, cols], second[:, cols]
        held.append(jnp.concatenate([jnp.where(even, one, two), jnp.where(even, two, one)], axis=0))
    parts = columns_part(held, operator)
    for j in range(blocks):
        at = j * 2 * TILE
        south = pltpu.roll(held[j + 1][:TILE], HALO, 0)
        north = pltpu.roll(held[j + 1][TILE:], HALO, 0)
        for d in range(1, HALO):
            part = parts[at : at + 2 * TILE, (d - 1) * LANES : d * LANES]
            south += jnp.where(place >= HALO - d, pltpu.roll(part[:TILE], TILE - d, 0), zero)
            north += jnp.where(place < d, pltpu.roll(part[TILE:], d, 0), zero)
        south = south * south_scale
        north = north * north_scale
        for day in range(days):
            north_day = north if day == 0 else pltpu.roll(north, HALO, 0)
            south_day = south if day == 0 else pltpu.roll(south, HALO, 0)
            out[j, day, :TILE] = own[j, day, :TILE] + jnp.where(low, north_day, zero)
            out[j, day, TILE : rows - TILE] = own[j, day, TILE : rows - TILE]
            out[j, day, rows - TILE :] = own[j, day, rows - TILE :] + jnp.where(low, zero, south_day)


def stack_left(matrix):
    high, low = split(matrix)
    return jnp.concatenate([high, low, high], axis=1)


def maps_kernel(predictors, inverse_gram, to_coefficients, to_fitted):
    scores = predictors[...]
    contract = (((1,), (1,)), ((), ()))
    direct = lax.dot_general(
        inverse_gram[...], scores, contract, precision=HIGHEST, preferred_element_type=jnp.float32
    )
    back = jnp.dot(scores, direct, precision=HIGHEST, preferred_element_type=jnp.float32)
    to_coefficients[...] = stack_left(direct)
    to_fitted[...] = stack_left(back)


def pairs(smooth, rows, days):
    for r in range(0, rows, 2):
        high, low = split(jnp.concatenate([smooth[pl.ds(r + i, days, stride=rows), :] for i in range(2)], axis=1))
        yield r, jnp.concatenate([high, high, low], axis=0)


def fitted_kernel(smooth, matrix, fitted):
    days = matrix.shape[0]
    rows = smooth.shape[0] // days
    for r, right in pairs(smooth, rows, days):
        both = jnp.dot(matrix[...], right, preferred_element_type=jnp.float32)
        for i in range(2):
            fitted[pl.ds(r + i, days, stride=rows), :] = both[:, i * LANES : (i + 1) * LANES]


def proximal(obs, dual, fitted):
    shifted = obs + dual - fitted
    auxiliary = shifted - jnp.clip(shifted, -(1.0 - QUANTILE) / PENALTY, QUANTILE / PENALTY)
    return auxiliary, shifted - auxiliary


def sums_kernel(obs, aux, dual, fitted, sums):
    blocks, days, rows, _ = fitted.shape

    zero = jnp.zeros((rows, LANES), jnp.float32)
    totals = [[zero, zero] for _ in range(4)]
    for j in range(blocks):
        cols = pl.ds(j * LANES, LANES)
        for day in range(days):
            total = totals[(j * days + day) % len(totals)]
            dual_now = dual[day, :, cols]
            aux_new, dual_new = proximal(obs[day, :, cols], dual_now, fitted[j, day])
            moved = dual_new - dual_now
            total[0] += moved * moved
            moved = aux_new - aux[day, :, cols]
            total[1] += moved * moved
    primal = (totals[0][0] + totals[1][0]) + (totals[2][0] + totals[3][0])
    change = (totals[0][1] + totals[1][1]) + (totals[2][1] + totals[3][1])
    primal = jnp.sum(primal, axis=0, keepdims=True)
    change = jnp.sum(change, axis=0, keepdims=True)
    half = LANES // 2
    both = jnp.where(
        iota((1, LANES), 1) < half, primal + pltpu.roll(primal, half, 1), change + pltpu.roll(change, half, 1)
    )
    sums[...] = jnp.broadcast_to(both, sums.shape)


def results_kernel(
    smooth, matrix, obs, dual, fitted, after, coefficients, aux_next, dual_next, stacked, held, aux_held, dual_held, sems
):
    depth = matrix.shape[0]
    days_all = matrix.shape[1] // 3
    blocks, days, rows, _ = fitted.shape
    part = depth // PARTS
    copies = []

    def send(source, target, k):
        copies.append(pltpu.make_async_copy(source, target, sems.at[k]))
        copies[-1].start(priority=k % 2)

    for day in range(days):

        def body(group, carry):
            for u in range(UNROLL):
                j = group * UNROLL + u
                cols = pl.ds(pl.multiple_of(j * LANES, LANES), LANES)
                aux_new, dual_new = proximal(obs[day, :, cols], dual[day, :, cols], fitted[j, day])
                aux_held[day, :, cols] = aux_new
                dual_held[day, :, cols] = dual_new
            return carry

        lax.fori_loop(0, blocks // UNROLL, body, 0)
        send(aux_held.at[day], aux_next.at[day], PARTS + day)
        send(dual_held.at[day], dual_next.at[day], PARTS + days + day)

    for r, right in pairs(smooth, rows, days_all):
        stacked[r // 2] = right
    for k in range(PARTS):
        for r in range(0, rows, 2):
            both = jnp.dot(
                matrix[k * part : (k + 1) * part, :], stacked[r // 2], preferred_element_type=jnp.float32
            )
            for i in range(2):
                held[pl.ds(k * part * rows + r + i, part, stride=rows), :] = both[:, i * LANES : (i + 1) * LANES]
        span = pl.ds(k * part * rows, part * rows)
        send(held.at[span], coefficients.at[span], k)
    for copy in copies:
        copy.wait()


def norms_kernel(sums, primal, change):
    row = jnp.sum(sums[...], axis=0, keepdims=True)
    half = iota(row.shape, 1) < LANES // 2
    primal[...] = jnp.sqrt(jnp.sum(jnp.where(half, row, 0.0), axis=1, keepdims=True))
    change[...] = PENALTY * jnp.sqrt(jnp.sum(jnp.where(half, 0.0, row), axis=1, keepdims=True))


def local(lat_count, lon_count, observations, aux_state, dual_state, predictors, inverse_gram):
    days, rows, columns = observations.shape
    blocks = columns // LANES
    all_days = days * lon_count
    depth = inverse_gram.shape[0]
    field = f32(blocks, days, rows, LANES)
    state = (observations, aux_state, dual_state)
    slab = f32(days, rows, columns)
    tile = f32(TILE, columns)
    first, second = call(
        edges_kernel,
        (tile, tile),
        [IN_HBM] * 3,
        (IN_VMEM,) * 2,
        2.0,
        [pltpu.VMEM((2, 3, days, TILE, columns), jnp.float32), DMA((2, 3))],
        EDGES_MIB,
    )(*state)
    first = lax.ppermute(first, "lat", [(i, i ^ 1) for i in range(lat_count)])
    second = lax.ppermute(second, ("lat", "lon"), middle_pairs(lat_count, lon_count))
    own = call(functools.partial(own_kernel, lat_count), field, [IN_VMEM] * 4, IN_VMEM, 3.0)(
        *state, columns_operator(columns_bands()[:SWEEPS])
    )
    to_coefficients, to_fitted = call(
        maps_kernel,
        (bf16(depth, 3 * all_days), bf16(all_days, 3 * all_days)),
        [IN_VMEM] * 2,
        (IN_VMEM, IN_VMEM),
        2.0,
    )(predictors, inverse_gram)
    smooth = call(functools.partial(halo_kernel, lat_count), field, [IN_VMEM] * 5, IN_VMEM, 1.5)(
        own, second, first, columns_operator(distance_bands()), to_fitted
    )
    smooth = lax.all_to_all(smooth, "lon", 0, 0, tiled=True).reshape(all_days * rows, LANES)
    fitted = call(fitted_kernel, f32(all_days * rows, LANES), [IN_VMEM] * 2, IN_VMEM, 2.0)(smooth, to_fitted)
    fitted = lax.all_to_all(fitted.reshape(field.shape), "lon", 0, 0, tiled=True)
    devices = lat_count * lon_count
    sums = call(sums_kernel, f32(1, LANES), [IN_VMEM] * 4, IN_VMEM, 1.0)(
        *state, fitted
    )
    coefficients, aux_next, dual_next = call(
        results_kernel,
        (f32(depth * rows, LANES), slab, slab),
        [IN_VMEM] * 5 + [IN_HBM],
        (IN_HBM,) * 3,
        5.0,
        [
            pltpu.VMEM((rows // 2, 3 * all_days, 2 * LANES), jnp.bfloat16),
            pltpu.VMEM((depth * rows, LANES), jnp.float32),
            pltpu.VMEM(slab.shape, jnp.float32),
            pltpu.VMEM(slab.shape, jnp.float32),
            DMA((PARTS + 2 * days,)),
        ],
    )(smooth, to_coefficients, observations, dual_state, fitted, sums)
    coefficients = coefficients.reshape(depth, rows, LANES)
    sums = jnp.broadcast_to(sums[None], (devices, 1, LANES))
    sums = lax.all_to_all(sums, ("lat", "lon"), 0, 0, tiled=True).reshape(devices, LANES)
    primal, change = call(norms_kernel, (f32(1, 1), f32(1, 1)), [IN_VMEM], (IN_VMEM, IN_VMEM), 0.5)(sums)
    return (coefficients, aux_next, dual_next, primal.reshape(()), change.reshape(()))


def solution(mesh):
    in_specs = (P("lon", "lat", None), P("lon", "lat", None), P("lon", "lat", None), P(), P())
    out_specs = (P(None, "lat", "lon"), P("lon", "lat", None), P("lon", "lat", None), P(), P())
    body = functools.partial(local, mesh.shape["lat"], mesh.shape["lon"])
    return jax.shard_map(body, mesh=mesh, in_specs=in_specs, out_specs=out_specs, check_vma=False)
```
